128 devices in a mesh: row: 32 (over z, y, core), col: 4 (over x).
Axes of the slice: x: 4, y: 4, z: 4, core: 2. Of those that a mesh axis runs over, the one named last changes fastest.
Arguments:
- blocks: bfloat16 [4, 32, 128, 32, 4, 128], P(None, 'row', None, None, 'col'), may hold values from -5 to 5, as said below
- scales: float32 [4, 32, 32, 4], P(None, 'row', None, 'col'), may hold values from 0 to 3, as said below
Outputs:
- factored: bfloat16 [4, 32, 128, 32, 4, 128], P(None, 'row', None, None, 'col')
- block_scales: float32 [4, 32, 32, 4], P(None, 'row', None, 'col')
The draws below stay inside these ranges and needn't reach their ends.
Inputs may be any that keep to these rules, and one draw needn't show every extreme that they name: blocks times scales form a symmetric positive definite matrix; scales of block (I, J) and (J, I) are equal, and so are the blocks up to transposition. `scales`: positive.
All inputs are finite; a program needn't handle non-finite values. Where the reference program divides by a largest or mean magnitude, that divisor is 1e-20 or more.
Results may differ from the reference program's by a relative error of at most 0.0044.
Values may be sent and summed in bfloat16 or wider, within the bound.
No kernel may reach another device: no remote copies, remote signals or barrier semaphores. Data moves between devices by JAX's collectives and lax.ppermute only.
A program may use at most 128 MiB of HBM per device.

```python
import math
import jax
import jax.numpy as jnp
from jax import lax

RB = 4
BS = 128
CB = 32
N_ROW = 32
N_COL = 4


def strong_links(key, positions, order):
    linked = jnp.zeros((order, order), jnp.float32)
    for matching in range(3):
        key_perm, key_strength, key_polarity = jax.random.split(jax.random.fold_in(key, matching), 3)
        shuffled = jax.random.permutation(key_perm, order)
        paired = shuffled.reshape(order // 2, 2)
        strength = jnp.exp(jax.random.uniform(key_strength, (order // 2,), jnp.float32, math.log(0.2), math.log(0.45)))
        polarity = jnp.where(jax.random.bernoulli(key_polarity, 0.5, (order // 2,)), 1.0, -1.0)
        weight = strength * polarity
        partner = jnp.zeros((order,), jnp.int32).at[paired[:, 0]].set(paired[:, 1]).at[paired[:, 1]].set(paired[:, 0])
        node_weight = jnp.zeros((order,), jnp.float32).at[paired[:, 0]].set(weight).at[paired[:, 1]].set(weight)
        linked = linked + jnp.where(partner[:, None] == positions[None, :], node_weight[:, None], 0.0)
    return linked


def symmetric_system(key):
    order = RB * N_ROW * BS
    count = RB * N_ROW
    key_main, key_diag, key_scale, key_direction, key_polarity, key_links = jax.random.split(jax.random.fold_in(key, 7), 6)
    values = jnp.clip(jax.random.normal(key_main, (order, order), jnp.float32), -4.0, 4.0)
    sym_values = jnp.clip((values + values.T) * 0.7071, -5.0, 5.0)
    positions = jnp.arange(order)
    block_ids = positions // BS
    same_block = block_ids[:, None] == block_ids[None, :]
    on_diag = positions[:, None] == positions[None, :]
    diag_values = jax.random.uniform(key_diag, (order,), jnp.float32, 4.5, 6.5)
    noise = jnp.where(same_block, sym_values * 0.03, sym_values * 0.006)
    magnitude = jax.random.uniform(key_direction, (order,), jnp.float32, 0.5, 1.0)
    polarity = jnp.where(jax.random.bernoulli(key_polarity, 0.5, (order,)), 1.0, -1.0)
    direction = (magnitude * polarity).astype(jnp.bfloat16).astype(jnp.float32)
    coherent = direction[:, None] * direction[None, :] * 0.25
    linked = strong_links(key_links, positions, order)
    matrix = jnp.where(on_diag, diag_values[:, None] + coherent, noise + coherent + linked)
    logs = jax.random.uniform(key_scale, (count, count), jnp.float32, math.log(0.35), math.log(0.7))
    index_rows = jnp.arange(count)[:, None]
    index_cols = jnp.arange(count)[None, :]
    logs = jnp.where(index_rows <= index_cols, logs, logs.T)
    block_scale = jnp.where(index_rows == index_cols, 4.0 * jnp.exp(logs), jnp.exp(logs))
    stored = matrix.reshape(count, BS, count, BS) / block_scale[:, None, :, None]
    stored = jnp.clip(stored, -5.0, 5.0).reshape(order, order)
    return (stored, block_scale)


def draw_blocks(key, part):
    stored, block_scale = symmetric_system(key)
    return stored.reshape(RB, N_ROW, BS, CB, N_COL, BS).astype(jnp.bfloat16)


def draw_scales(key, part):
    stored, block_scale = symmetric_system(key)
    return block_scale.reshape(RB, N_ROW, CB, N_COL).astype(jnp.float32)


def setup_inputs(seed: int = 0) -> dict:
    key_list = jax.random.split(jax.random.key(seed), 3)
    blocks = draw_blocks(jax.random.fold_in(key_list[2], 71), 0)
    scales = draw_scales(jax.random.fold_in(key_list[2], 71), 0)
    return dict(blocks=blocks, scales=scales)


def reference(blocks, scales):
    order = RB * N_ROW * BS
    matrix = (blocks.astype(jnp.float32) * scales[:, :, None, :, :, None]).reshape(order, order)
    factors = []
    strips = []
    for panel in range(2):
        start = panel * BS
        finish = start + BS
        factor = jnp.linalg.cholesky(matrix[start:finish, start:finish])
        below = matrix[finish:, start:finish]
        solved = lax.linalg.triangular_solve(factor, below, left_side=False, lower=True, transpose_a=True)
        strip = solved.astype(jnp.bfloat16)
        product = jnp.dot(strip.astype(jnp.float32), strip.T.astype(jnp.float32), preferred_element_type=jnp.float32)
        matrix = matrix.at[finish:, finish:].add(-product)
        factors.append(factor)
        strips.append(strip)
    for panel in range(2):
        start = panel * BS
        finish = start + BS
        matrix = matrix.at[start:finish, start:finish].set(factors[panel])
        matrix = matrix.at[finish:, start:finish].set(strips[panel].astype(jnp.float32))
        matrix = matrix.at[start:finish, finish:].set(strips[panel].T.astype(jnp.float32))
    shaped = matrix.reshape(RB, N_ROW, BS, CB, N_COL, BS)
    largest = jnp.max(jnp.abs(shaped), axis=(2, 5)) + 1e-06
    factored = (shaped / largest[:, :, None, :, :, None]).astype(jnp.bfloat16)
    return (factored, largest)
```

```python
import jax
import jax.numpy as jnp
from jax import lax
from jax.experimental import pallas as pl
from jax.experimental.pallas import tpu as pltpu
from jax.sharding import PartitionSpec as P

AXES = ("row", "col")
NX, NY, NZ, NK = 4, 4, 4, 2
BS = 128
PIECE = 4 * BS + 16
HIGH = lax.Precision.HIGHEST


def dev(z, y, k, x):
    return (((z % NZ) * NY + (y % NY)) * NK + (k % NK)) * NX + (x % NX)


PLACES = [(z, y, k, x) for z in range(NZ) for y in range(NY) for k in range(NK) for x in range(NX)]


def shift(array, dz=0, dy=0, dk=0, dx=0, where=lambda z, y, k, x: True):
    pairs = [
        (dev(z, y, k, x), dev(z + dz, y + dy, k + dk, x + dx)) for z, y, k, x in PLACES if where(z, y, k, x)
    ]
    return lax.ppermute(array, AXES, pairs)


def scale_rows(scale):
    high = lax.reduce_precision(scale, 8, 7)
    rest = scale - high
    mid = lax.reduce_precision(rest, 8, 7)
    low = lax.reduce_precision(rest - mid, 8, 7)
    rows = jnp.stack([high, mid, low], axis=1).reshape(12, 1)
    rows = jnp.concatenate([rows, jnp.zeros((4, 1), jnp.float32)], axis=0)
    return jnp.broadcast_to(rows, (16, BS)).astype(jnp.bfloat16)


def along_x(array, x, where=lambda z, y, k, x: True):
    pairs = [
        [(0, 1), (1, 0)],
        [(0, 3), (1, 2)],
        [(0, 2), (1, 3)],
    ]
    got = []
    for hop in pairs:
        table = [
            (dev(z, y, k, s), dev(z, y, k, t))
            for z, y, k, s in PLACES
            for s0, t in hop
            if s == s0 and where(z, y, k, s)
        ]
        got.append(lax.ppermute(array, AXES, table))
    u = jnp.where(x <= 1, array, got[1])
    v = jnp.where(x <= 1, got[0], got[2])
    return u, v


def leading_block(lead, z, y, k, x):
    at_root = lambda z, y, k, x: z == 0 and y == 0 and (k == 1 or x == 0)
    u, v = along_x(lead, x, at_root)
    first = (x == 0) | (x == 3)
    pair = jnp.concatenate([jnp.where(first, u, v), jnp.where(first, v, u)], axis=0)
    root = lambda z, y, k, x: z == 0 and y == 0
    up, down, over = (shift(pair, dy=d, where=root) for d in (1, -1, 2))
    pair = jnp.where(y == 0, pair, jnp.where(y == 1, up, jnp.where(y == 3, down, over)))
    root = lambda z, y, k, x: z == 0
    up, down, over = (shift(pair, dz=d, where=root) for d in (1, -1, 2))
    pair = jnp.where(z == 0, pair, jnp.where(z == 1, up, jnp.where(z == 3, down, over)))
    other = shift(pair, dk=1)
    rows = BS + 16
    core0 = jnp.where(k == 0, pair, other)
    core1 = jnp.where(k == 0, other, pair)
    blocks = [core0[:rows], core1[:rows], core1[rows:]]

    def value(b):
        s = b[BS].astype(jnp.float32) + b[BS + 1].astype(jnp.float32) + b[BS + 2].astype(jnp.float32)
        return b[:BS].astype(jnp.float32) * s[None, :]

    return [value(b) for b in blocks]


def column_pieces(piece, z, y, k, x):
    table = [
        (dev(zz, yy, kk, p), dev(zz, yy, p, 2 * (yy % 2) + kk))
        for zz in range(NZ)
        for yy in range(NY)
        for kk in range(NK)
        for p in range(2)
    ]
    mine = lax.ppermute(piece, AXES, table)
    source = lambda z, y, k, x: y % 2 == x // 2
    up, down, over = (shift(mine, dy=d, where=source) for d in (1, -1, 2))
    turn = (y - x // 2) % 4
    slot0 = jnp.where(turn == 0, mine, jnp.where(turn == 1, up, jnp.where(turn == 2, over, down)))
    slot1 = jnp.where(turn == 0, over, jnp.where(turn == 1, down, jnp.where(turn == 2, mine, up)))
    both = jnp.concatenate([slot0, slot1], axis=0)
    held = [both] + [shift(both, dz=d) for d in (1, -1, 2)]
    return held, [shift(h, dk=1) for h in held]


def factor(blocks):
    d00, d10, d11 = blocks
    eye = jnp.eye(BS, dtype=jnp.float32)
    solve = lambda l: lax.linalg.triangular_solve(l, eye, left_side=True, lower=True)
    l0 = jnp.linalg.cholesky(d00)
    w00 = solve(l0)
    l10 = jnp.dot(d10, w00.T, precision=HIGH).astype(jnp.bfloat16)
    l10f = l10.astype(jnp.float32)
    l1 = jnp.linalg.cholesky(d11 - jnp.dot(l10f, l10f.T, precision=HIGH))
    w11 = solve(l1)
    w10 = -jnp.dot(w11, jnp.dot(l10f, w00, precision=HIGH), precision=HIGH)
    wt = jnp.concatenate(
        [
            jnp.concatenate([w00.T, w10.T], axis=1),
            jnp.concatenate([jnp.zeros_like(eye), w11.T], axis=1),
        ],
        axis=0,
    )
    return l0, l10f, l1, wt


def finish_kernel(place, a_ref, sc_ref, m0, m1, m2, m3, t0, t1, t2, t3, u_ref, v_ref, wt_ref, corner_ref,
                  out_ref, big_ref, q_ref, p_ref, prod_ref, wk_ref):
    step = pl.program_id(0)
    row, col, k, z, first = place[0], place[1], place[2], place[3], place[4]

    def scale_of(ref, base, a):
        s = ref[base + 4 * BS : base + 4 * BS + 16, :].astype(jnp.float32)
        return s[3 * a : 3 * a + 1] + s[3 * a + 1 : 3 * a + 2] + s[3 * a + 2 : 3 * a + 3]

    def panel_tile(ref_m, ref_t, base, a, wm, wt):
        def part(ref, w):
            raw = ref[base + a * BS : base + (a + 1) * BS, :]
            d = jnp.dot(jnp.concatenate([raw, raw], axis=1), w, preferred_element_type=jnp.float32)
            s = scale_of(ref, base, a)
            return d * jnp.concatenate([s, s], axis=1)

        return (part(ref_m, wm) + part(ref_t, wt)).astype(jnp.bfloat16)

    @pl.when(step == 0)
    def _():
        w = wt_ref[...]
        hi = w.astype(jnp.bfloat16)
        lo = (w - hi.astype(jnp.float32)).astype(jnp.bfloat16)
        for h in range(2):
            wk_ref[h, :BS, :] = hi[h * BS : (h + 1) * BS]
            wk_ref[h, BS:, :] = lo[h * BS : (h + 1) * BS]
        w_mine = wk_ref[k]
        w_other = wk_ref[1 - k]
        for i, (mine, other) in enumerate(((m0, t0), (m1, t1), (m2, t2), (m3, t3))):
            zs = lax.rem(z + (0, 3, 1, 2)[i], 4)
            for ys in range(2):
                for a in range(4):
                    b = a * 8 + zs * 2 + ys
                    q_ref[pl.ds(pl.multiple_of(b * BS, BS), BS), :] = panel_tile(
                        mine, other, ys * PIECE, a, w_mine, w_other
                    )
        w_u = wk_ref[first]
        w_v = wk_ref[1 - first]
        for a in range(4):
            p_ref[a * BS : (a + 1) * BS, :] = panel_tile(u_ref, v_ref, 0, a, w_u, w_v)
        e = lax.broadcasted_iota(jnp.int32, (BS, 2 * BS), 0)
        f = lax.broadcasted_iota(jnp.int32, (BS, 2 * BS), 1)

        @pl.when(row < 2)
        def _():
            p_ref[0:BS, :] = jnp.where(f == e + row * BS, -1.0, 0.0).astype(jnp.bfloat16)

        @pl.when(col < 2)
        def _():
            q_ref[0:BS, :] = jnp.where(f == e + col * BS, -1.0, 0.0).astype(jnp.bfloat16)

    p = p_ref[pl.ds(pl.multiple_of(step * BS, BS), BS), :]
    for b in range(32):
        d = lax.dot_general(
            p, q_ref[b * BS : (b + 1) * BS, :], (((1,), (1,)), ((), ())), preferred_element_type=jnp.float32
        )
        prod_ref[pl.ds(b, BS, stride=32), :] = d

    @pl.when((step == 0) & (row < 2) & (col < 2))
    def _():
        prod_ref[pl.ds(0, BS, stride=32), :] = -corner_ref[...]

    sc = sc_ref[0]

    def update(e, mx):
        rows = pl.ds(pl.multiple_of(e * 32, 32), 32)
        m = a_ref[0, e].astype(jnp.float32) * sc - prod_ref[rows, :]
        prod_ref[rows, :] = m
        return jnp.maximum(mx, jnp.abs(m))

    mx = lax.fori_loop(0, BS, update, jnp.zeros((32, BS), jnp.float32), unroll=8)
    big = jnp.max(mx, axis=1, keepdims=True) + 1e-06
    big = jnp.broadcast_to(big, (32, BS))
    big_ref[0] = big
    inv = 1.0 / big

    def divide(e, carry):
        rows = pl.ds(pl.multiple_of(e * 32, 32), 32)
        out_ref[0, e] = (prod_ref[rows, :] * inv).astype(jnp.bfloat16)
        return carry

    lax.fori_loop(0, BS, divide, 0, unroll=8)


def finish(place, blocks, sc, held, others, u, v, wt, corner):
    whole = lambda shape: pl.BlockSpec(shape, lambda a, *_: (0,) * len(shape))
    spec = pltpu.PrefetchScalarGridSpec(
        num_scalar_prefetch=1,
        grid=(4,),
        in_specs=[
            pl.BlockSpec((1, BS, 32, BS), lambda a, *_: (a, 0, 0, 0)),
            pl.BlockSpec((1, 32, BS), lambda a, *_: (a, 0, 0)),
        ]
        + [whole((2 * PIECE, BS))] * 8
        + [whole((PIECE, BS))] * 2
        + [whole((2 * BS, 2 * BS)), whole((BS, BS))],
        out_specs=[
            pl.BlockSpec((1, BS, 32, BS), lambda a, *_: (a, 0, 0, 0)),
            pl.BlockSpec((1, 32, BS), lambda a, *_: (a, 0, 0)),
        ],
        scratch_shapes=[
            pltpu.VMEM((32 * BS, 2 * BS), jnp.bfloat16),
            pltpu.VMEM((4 * BS, 2 * BS), jnp.bfloat16),
            pltpu.VMEM((32 * BS, BS), jnp.float32),
            pltpu.VMEM((2, 2 * BS, 2 * BS), jnp.bfloat16),
        ],
    )
    return pl.pallas_call(
        finish_kernel,
        grid_spec=spec,
        out_shape=[
            jax.ShapeDtypeStruct((4, BS, 32, BS), jnp.bfloat16),
            jax.ShapeDtypeStruct((4, 32, BS), jnp.float32),
        ],
        compiler_params=pltpu.CompilerParams(vmem_limit_bytes=32 * 1024 * 1024),
        cost_estimate=pl.CostEstimate(flops=2 * 512 * 4096 * 512, bytes_accessed=12 * 2**20, transcendentals=0),
        name="finish",
    )(place, blocks, sc, *held, *others, u, v, wt, corner)


def on_device(blocks, scales):
    row = lax.axis_index("row")
    col = lax.axis_index("col")
    x = col
    k = row % 2
    y = (row // 2) % 4
    z = row // 8
    blocks = blocks.reshape(4, BS, 32, BS)
    scales = scales.reshape(4, 32)
    srows = scale_rows(scales[:, 0])
    strip = blocks[:, :, 0, :]
    piece = jnp.concatenate([strip.reshape(4 * BS, BS), srows], axis=0)
    lead = jnp.concatenate([strip[0], srows], axis=0)

    lead_blocks = leading_block(lead, z, y, k, x)
    held, others = column_pieces(piece, z, y, k, x)
    u, v = along_x(piece, x)
    l0, l10, l1, wt = factor(lead_blocks)
    corner = jnp.where(
        row == 0, jnp.where(col == 0, l0, l10.T), jnp.where(col == 0, l10, l1)
    )
    special = ((jnp.arange(4) == 0) & (row < 2))[:, None] | ((jnp.arange(32) == 0) & (col < 2))[None, :]
    sc = jnp.broadcast_to(jnp.where(special, 0.0, scales)[:, :, None], (4, 32, BS))
    first = jnp.where((x == 0) | (x == 3), 0, 1)
    place = jnp.stack([row, col, k, z, first]).astype(jnp.int32)
    factored, largest = finish(place, blocks, sc, held, others, u, v, wt, corner)
    return factored.reshape(4, 1, BS, 32, 1, BS), largest[:, None, :, :1]


def solution(mesh):
    in_specs = (P(None, "row", None, None, "col", None), P(None, "row", None, "col"))
    out_specs = (P(None, "row", None, None, "col", None), P(None, "row", None, "col"))
    return jax.shard_map(
        on_device, mesh=mesh, in_specs=in_specs, out_specs=out_specs, check_vma=False
    )
```

```python
import jax
import jax.numpy as jnp
from jax import lax
from jax.experimental import pallas as pl
from jax.experimental.pallas import tpu as pltpu
from jax.sharding import PartitionSpec as P

AXES = ("row", "col")
NX, NY, NZ, NK = 4, 4, 4, 2
BS = 128
PIECE = 4 * BS + 16


def dev(z, y, k, x):
    return (((z % NZ) * NY + (y % NY)) * NK + (k % NK)) * NX + (x % NX)


PLACES = [(z, y, k, x) for z in range(NZ) for y in range(NY) for k in range(NK) for x in range(NX)]


def shift(array, dz=0, dy=0, dk=0, dx=0, where=lambda z, y, k, x: True):
    pairs = [
        (dev(z, y, k, x), dev(z + dz, y + dy, k + dk, x + dx)) for z, y, k, x in PLACES if where(z, y, k, x)
    ]
    return lax.ppermute(array, AXES, pairs)


def scale_rows(scale):
    high = lax.reduce_precision(scale, 8, 7)
    rest = scale - high
    mid = lax.reduce_precision(rest, 8, 7)
    low = lax.reduce_precision(rest - mid, 8, 7)
    rows = jnp.stack([high, mid, low], axis=1).reshape(12, 1)
    rows = jnp.concatenate([rows, jnp.zeros((4, 1), jnp.float32)], axis=0)
    return jnp.broadcast_to(rows, (16, BS)).astype(jnp.bfloat16)


def along_x(array, x):
    got = []
    for hop in ({0: 1, 1: 0}, {0: 3, 1: 2}, {0: 2, 1: 3}):
        table = [(dev(z, y, k, s), dev(z, y, k, hop[s])) for z, y, k, s in PLACES if s in hop]
        got.append(lax.ppermute(array, AXES, table))
    u = jnp.where(x <= 1, array, got[1])
    v = jnp.where(x <= 1, got[0], got[2])
    return u, v


def leading_pair(u, v, first, z, y):
    head = lambda w: jnp.concatenate([w[:BS], w[4 * BS :]], axis=0)
    pair = jnp.concatenate([jnp.where(first == 0, head(u), head(v)), jnp.where(first == 0, head(v), head(u))], axis=0)
    root = lambda z, y, k, x: z == 0 and y == 0
    up, down, over = (shift(pair, dy=d, where=root) for d in (1, -1, 2))
    pair = jnp.where(y == 0, pair, jnp.where(y == 1, up, jnp.where(y == 3, down, over)))
    root = lambda z, y, k, x: z == 0
    up, down, over = (shift(pair, dz=d, where=root) for d in (1, -1, 2))
    return jnp.where(z == 0, pair, jnp.where(z == 1, up, jnp.where(z == 3, down, over)))


def column_strips(u, v, first, y, k, x):
    source = lambda z, y, k, x: y % 2 == x // 2
    giver = lambda z, y, k, x: source(z, y, k, x) and k == x % 2
    ours = jnp.where(first == k, u, v)
    mine = jnp.where(k == x % 2, ours, shift(jnp.where(first == k, v, u), dk=1, where=giver))
    up, down, over = (shift(mine, dy=d, where=source) for d in (1, -1, 2))
    turn = (y - x // 2) % 4
    slot0 = jnp.where(turn == 0, mine, jnp.where(turn == 1, up, jnp.where(turn == 2, over, down)))
    slot1 = jnp.where(turn == 0, over, jnp.where(turn == 1, down, jnp.where(turn == 2, mine, up)))
    return jnp.concatenate([slot0, slot1], axis=0)


def split3(x):
    h = x.astype(jnp.bfloat16).astype(jnp.float32)
    m = (x - h).astype(jnp.bfloat16).astype(jnp.float32)
    return h, m, x - h - m


def splat(x, shape):
    return jnp.broadcast_to(x, shape)


def eliminate(ref):
    width = ref.shape[1]
    lanes = width // BS
    wide = lambda w: jnp.concatenate([w] * lanes, axis=1)
    for base in range(0, BS, 8):
        tile = ref[base : base + 8, :]
        rows = [splat(tile[i : i + 1, :], (8, width)) for i in range(8)]
        cols = [splat(tile[:, base + j : base + j + 1], (8, BS)) for j in range(8)]
        e = [[splat(cols[j][i : i + 1, :], (8, BS)) for j in range(i + 1)] for i in range(8)]
        for j in range(8):
            r = lax.rsqrt(e[j][j])
            rows[j] = rows[j] * wide(r)
            l = [None] * 8
            for i in range(j + 1, 8):
                l[i] = e[i][j] * r
            for i in range(j + 1, 8):
                for m in range(j + 1, i + 1):
                    e[i][m] = e[i][m] - l[i] * l[m]
                rows[i] = rows[i] - wide(l[i]) * rows[j]
        sub = lax.broadcasted_iota(jnp.int32, (8, width), 0)
        out = rows[0]
        for i in range(1, 8):
            out = jnp.where(sub == i, rows[i], out)
        below = lax.broadcasted_iota(jnp.int32, (8, BS), 0) + base
        upper = jnp.where(lax.broadcasted_iota(jnp.int32, (8, BS), 1) >= below, out[:, :BS], 0.0)
        out = jnp.concatenate([upper, out[:, BS:]], axis=1)
        ref[base : base + 8, :] = out
        if base + 8 < BS:
            h, m, l = split3(out)
            left = jnp.concatenate([w[:, :BS] for w in (h, h, m, m, h, l)], axis=0).astype(jnp.bfloat16)
            right = jnp.concatenate([h, m, h, m, l, h], axis=0).astype(jnp.bfloat16)
            d = lax.dot_general(left, right, (((0,), (0,)), ((), ())), preferred_element_type=jnp.float32)
            ref[base + 8 :, :] = ref[base + 8 :, :] - d[base + 8 :, :]


def factor_kernel(place, pair_ref, other_ref, wk_ref, corner_ref, one_ref, two_ref):
    row, col, k = place[0], place[1], place[2]
    rows = BS + 16

    def value(ref, base):
        s = ref[base + BS : base + rows, :].astype(jnp.float32)
        s = s[0:1] + s[1:2] + s[2:3]
        return ref[base : base + BS, :].astype(jnp.float32) * s

    def fill(core0, core1):
        one_ref[:, :BS] = value(core0, 0)
        one_ref[:, BS : 2 * BS] = value(core1, 0).T
        two_ref[:, :BS] = value(core1, rows)

    @pl.when(k == 0)
    def _():
        fill(pair_ref, other_ref)

    @pl.when(k == 1)
    def _():
        fill(other_ref, pair_ref)

    e = lax.broadcasted_iota(jnp.int32, (BS, BS), 0)
    f = lax.broadcasted_iota(jnp.int32, (BS, BS), 1)
    eye = jnp.where(e == f, 1.0, 0.0)
    one_ref[:, 2 * BS :] = eye
    eliminate(one_ref)
    l10t = one_ref[:, BS : 2 * BS].astype(jnp.bfloat16)
    w00 = one_ref[:, 2 * BS :]
    inner = (((0,), (0,)), ((), ()))
    two_ref[:, :BS] = two_ref[:, :BS] - lax.dot_general(l10t, l10t, inner, preferred_element_type=jnp.float32)
    two_ref[:, BS : 2 * BS] = eye
    parts = jnp.concatenate(split3(w00), axis=0).astype(jnp.bfloat16)
    two_ref[:, 2 * BS :] = -lax.dot_general(
        jnp.concatenate([l10t] * 3, axis=0), parts, inner, preferred_element_type=jnp.float32
    )
    eliminate(two_ref)

    def put(h, r, w):
        hi = w.astype(jnp.bfloat16)
        wk_ref[h, r * BS : (r + 1) * BS, :BS] = hi
        wk_ref[h, r * BS : (r + 1) * BS, BS:] = (w - hi.astype(jnp.float32)).astype(jnp.bfloat16)

    put(0, 0, w00)
    put(0, 1, two_ref[:, 2 * BS :])
    put(1, 0, jnp.zeros((BS, BS), jnp.float32))
    put(1, 1, two_ref[:, BS : 2 * BS])

    corner_ref[...] = l10t.astype(jnp.float32)

    @pl.when((row == 0) & (col == 0))
    def _():
        corner_ref[...] = one_ref[:, :BS].T

    @pl.when((row == 1) & (col == 0))
    def _():
        corner_ref[...] = l10t.astype(jnp.float32).T

    @pl.when((row == 1) & (col == 1))
    def _():
        corner_ref[...] = two_ref[:, :BS].T


def factor(place, pair, other):
    return pl.pallas_call(
        factor_kernel,
        grid_spec=pltpu.PrefetchScalarGridSpec(
            num_scalar_prefetch=1,
            in_specs=[pl.BlockSpec(memory_space=pltpu.VMEM)] * 2,
            out_specs=[pl.BlockSpec(memory_space=pltpu.VMEM)] * 2,
            scratch_shapes=[pltpu.VMEM((BS, 3 * BS), jnp.float32)] * 2,
        ),
        out_shape=[
            jax.ShapeDtypeStruct((2, 2 * BS, 2 * BS), jnp.bfloat16),
            jax.ShapeDtypeStruct((BS, BS), jnp.float32),
        ],
        compiler_params=pltpu.CompilerParams(vmem_limit_bytes=16 * 1024 * 1024),
        cost_estimate=pl.CostEstimate(flops=2 * 10**10, bytes_accessed=2**20, transcendentals=0),
        name="factor",
    )(place, pair, other)


def finish_kernel(place, a_ref, sc_ref, m0, m1, m2, m3, t0, t1, t2, t3, u_ref, v_ref, wk_ref, corner_ref,
                  out_ref, big_ref, q_ref, p_ref, prod_ref):
    step = pl.program_id(0)
    row, col, k, z, first = place[0], place[1], place[2], place[3], place[4]

    def scale_of(ref, base, a):
        s = ref[base + 4 * BS : base + 4 * BS + 16, :].astype(jnp.float32)
        return s[3 * a : 3 * a + 1] + s[3 * a + 1 : 3 * a + 2] + s[3 * a + 2 : 3 * a + 3]

    def panel_tiles(ref_m, ref_t, base, a0, wm, wt):
        def part(ref, w):
            raw = ref[base + a0 * BS : base + (a0 + 2) * BS, :]
            d = lax.dot_general(
                jnp.concatenate([raw, raw], axis=1), w, (((1,), (1,)), ((), ())), preferred_element_type=jnp.float32
            )
            out = []
            for a in range(2):
                s = scale_of(ref, base, a0 + a)
                out.append(d[a * BS : (a + 1) * BS] * jnp.concatenate([s, s], axis=1))
            return out

        return [(g + h).astype(jnp.bfloat16) for g, h in zip(part(ref_m, wm), part(ref_t, wt))]

    @pl.when(step == 0)
    def _():
        w_mine = wk_ref[k]
        w_other = wk_ref[1 - k]
        for i, (mine, other) in enumerate(((m0, t0), (m1, t1), (m2, t2), (m3, t3))):
            zs = lax.rem(z + (0, 3, 1, 2)[i], 4)
            for ys in range(2):
                for a0 in range(0, 4, 2):
                    tiles = panel_tiles(mine, other, ys * PIECE, a0, w_mine, w_other)
                    for a, tile in enumerate(tiles):
                        b = (a0 + a) * 8 + zs * 2 + ys
                        q_ref[pl.ds(pl.multiple_of(b * BS, BS), BS), :] = tile
        w_u = wk_ref[first]
        w_v = wk_ref[1 - first]
        for a0 in range(0, 4, 2):
            for a, tile in enumerate(panel_tiles(u_ref, v_ref, 0, a0, w_u, w_v)):
                p_ref[(a0 + a) * BS : (a0 + a + 1) * BS, :] = tile
        e = lax.broadcasted_iota(jnp.int32, (BS, 2 * BS), 0)
        f = lax.broadcasted_iota(jnp.int32, (BS, 2 * BS), 1)

        @pl.when(row < 2)
        def _():
            p_ref[0:BS, :] = jnp.where(f == e + row * BS, -1.0, 0.0).astype(jnp.bfloat16)

        @pl.when(col < 2)
        def _():
            q_ref[0:BS, :] = jnp.where(f == e + col * BS, -1.0, 0.0).astype(jnp.bfloat16)

    p = p_ref[pl.ds(pl.multiple_of(step * BS, BS), BS), :]
    for b in range(32):
        d = lax.dot_general(
            p, q_ref[b * BS : (b + 1) * BS, :], (((1,), (1,)), ((), ())), preferred_element_type=jnp.float32
        )
        prod_ref[pl.ds(b, BS, stride=40), :] = d

    @pl.when((step == 0) & (row < 2) & (col < 2))
    def _():
        prod_ref[pl.ds(0, BS, stride=40), :] = -corner_ref[...]

    sc = sc_ref[0]

    def update(e, mx):
        rows = pl.ds(pl.multiple_of(e * 40, 8), 32)
        m = a_ref[0, e].astype(jnp.float32) * sc - prod_ref[rows, :]
        prod_ref[rows, :] = m
        return jnp.maximum(mx, jnp.abs(m))

    mx = lax.fori_loop(0, BS, update, jnp.zeros((32, BS), jnp.float32), unroll=8)
    big = jnp.max(mx, axis=1, keepdims=True) + 1e-06
    big = jnp.broadcast_to(big, (32, BS))
    big_ref[0] = big
    inv = 1.0 / big

    def divide(e, carry):
        rows = pl.ds(pl.multiple_of(e * 40, 8), 32)
        out_ref[0, e] = (prod_ref[rows, :] * inv).astype(jnp.bfloat16)
        return carry

    lax.fori_loop(0, BS, divide, 0, unroll=8)


def finish(place, blocks, sc, held, others, u, v, wk, corner):
    whole = lambda shape: pl.BlockSpec(shape, lambda a, *_: (0,) * len(shape))
    spec = pltpu.PrefetchScalarGridSpec(
        num_scalar_prefetch=1,
        grid=(4,),
        in_specs=[
            pl.BlockSpec((1, BS, 32, BS), lambda a, *_: (a, 0, 0, 0)),
            pl.BlockSpec((1, 32, BS), lambda a, *_: (a, 0, 0)),
        ]
        + [whole((2 * PIECE, BS))] * 8
        + [whole((PIECE, BS))] * 2
        + [whole((2, 2 * BS, 2 * BS)), whole((BS, BS))],
        out_specs=[
            pl.BlockSpec((1, BS, 32, BS), lambda a, *_: (a, 0, 0, 0)),
            pl.BlockSpec((1, 32, BS), lambda a, *_: (a, 0, 0)),
        ],
        scratch_shapes=[
            pltpu.VMEM((32 * BS, 2 * BS), jnp.bfloat16),
            pltpu.VMEM((4 * BS, 2 * BS), jnp.bfloat16),
            pltpu.VMEM((40 * BS, BS), jnp.float32),
        ],
    )
    return pl.pallas_call(
        finish_kernel,
        grid_spec=spec,
        out_shape=[
            jax.ShapeDtypeStruct((4, BS, 32, BS), jnp.bfloat16),
            jax.ShapeDtypeStruct((4, 32, BS), jnp.float32),
        ],
        compiler_params=pltpu.CompilerParams(vmem_limit_bytes=32 * 1024 * 1024),
        cost_estimate=pl.CostEstimate(flops=2 * 512 * 4096 * 512, bytes_accessed=12 * 2**20, transcendentals=0),
        name="finish",
    )(place, blocks, sc, *held, *others, u, v, wk, corner)


def on_device(blocks, scales):
    row = lax.axis_index("row")
    col = lax.axis_index("col")
    x = col
    k = row % 2
    y = (row // 2) % 4
    z = row // 8
    blocks = blocks.reshape(4, BS, 32, BS)
    scales = scales.reshape(4, 32)
    srows = scale_rows(scales[:, 0])
    strip = blocks[:, :, 0, :]
    piece = jnp.concatenate([strip.reshape(4 * BS, BS), srows], axis=0)
    first = jnp.where((x == 0) | (x == 3), 0, 1)
    place = jnp.stack([row, col, k, z, first]).astype(jnp.int32)
    u, v = along_x(piece, x)
    pair = leading_pair(u, v, first, z, y)
    both = column_strips(u, v, first, y, k, x)
    pair, both = lax.optimization_barrier((pair, both))
    held = [both] + [shift(both, dz=d) for d in (1, -1, 2)]
    wk, corner = factor(place, pair, shift(pair, dk=1))
    wk, *held[1:] = lax.optimization_barrier((wk, *held[1:]))
    others = [shift(h, dk=1) for h in held]
    special = ((jnp.arange(4) == 0) & (row < 2))[:, None] | ((jnp.arange(32) == 0) & (col < 2))[None, :]
    sc = jnp.broadcast_to(jnp.where(special, 0.0, scales)[:, :, None], (4, 32, BS))
    factored, largest = finish(place, blocks, sc, held, others, u, v, wk, corner)
    return factored.reshape(4, 1, BS, 32, 1, BS), largest[:, None, :, :1]


def solution(mesh):
    in_specs = (P(None, "row", None, None, "col", None), P(None, "row", None, "col"))
    out_specs = (P(None, "row", None, None, "col", None), P(None, "row", None, "col"))
    return jax.shard_map(
        on_device, mesh=mesh, in_specs=in_specs, out_specs=out_specs, check_vma=False
    )
```

```python
import jax
import jax.numpy as jnp
from jax import lax
from jax.experimental import pallas as pl
from jax.experimental.pallas import tpu as pltpu
from jax.sharding import PartitionSpec as P

AXES = ("row", "col")
NX, NY, NZ, NK = 4, 4, 4, 2
BS = 128
PIECE = 4 * BS + 16


def dev(z, y, k, x):
    return (((z % NZ) * NY + (y % NY)) * NK + (k % NK)) * NX + (x % NX)


PLACES = [(z, y, k, x) for z in range(NZ) for y in range(NY) for k in range(NK) for x in range(NX)]


def permute(array, to):
    return lax.ppermute(array, AXES, [(dev(*place), dev(*to(*place))) for place in PLACES])


def sibling(z, y, k, x):
    return z, y, 1 - k, x


def strip_kernel(blocks_ref, scales_ref, piece_ref):
    sub = lax.broadcasted_iota(jnp.int32, (16, BS), 0)
    rows = jnp.zeros((16, BS), jnp.float32)
    for a in range(4):
        for t, part in enumerate(split3(jnp.broadcast_to(scales_ref[a, 0:1, 0:1], (16, BS)))):
            rows = jnp.where(sub == 3 * a + t, part, rows)
    rows = rows.astype(jnp.bfloat16)
    for a in range(4):
        piece_ref[a * BS : (a + 1) * BS, :] = blocks_ref[a, :, 0, :]
    piece_ref[4 * BS :, :] = rows


def strip(blocks, scales):
    return pl.pallas_call(
        strip_kernel,
        grid=(1,),
        in_specs=[
            pl.BlockSpec((4, BS, 16, BS), lambda i: (0, 0, 0, 0)),
            pl.BlockSpec((4, 1, 32), lambda i: (0, 0, 0)),
        ],
        out_specs=pl.BlockSpec((PIECE, BS), lambda i: (0, 0)),
        out_shape=jax.ShapeDtypeStruct((PIECE, BS), jnp.bfloat16),
        compiler_params=pltpu.CompilerParams(vmem_limit_bytes=60 * 1024 * 1024),
        cost_estimate=pl.CostEstimate(flops=0, bytes_accessed=2 * 2**20, transcendentals=0),
        name="strip",
    )(blocks, scales)


def along_x(array, x):
    got = [
        permute(array, lambda z, y, k, x: (z, y, k, hop[x])) for hop in ((1, 0, 3, 2), (3, 2, 1, 0), (2, 3, 0, 1))
    ]
    u = jnp.where(x <= 1, array, got[1])
    v = jnp.where(x <= 1, got[0], got[2])
    return u, v


def trade(p, q):
    return (q if p == 0 else 0), p in (0, q)


def pick(at, zero, one, two, three):
    return jnp.where(at == 0, zero, jnp.where(at == 1, one, jnp.where(at == 2, two, three)))


def along_y(mine, y, x):
    def across(z, y, k, x):
        return (z, y + 2, k, x) if y % 2 == x // 2 else (z, y, 1 - k, x)

    up = permute(mine, lambda z, y, k, x: (z, y + 1, k, x))
    down = permute(mine, lambda z, y, k, x: (z, y - 1, k, x))
    over = permute(mine, across)
    turn = (y - x // 2) % 4
    slots = [pick(turn, mine, up, over, down), pick(turn, over, down, mine, up)]
    return jnp.concatenate(slots, axis=0)


def lead_along(pair, at, axis):
    got = []
    for q in (1, 2, 3):

        def place(*here):
            there = list(here)
            other, moves = trade(here[axis], q)
            there[axis if moves else 2] = other if moves else 1 - here[2]
            return there

        got.append(permute(pair, place))
    return pick(at, pair, *got)


def split3(x):
    h = x.astype(jnp.bfloat16).astype(jnp.float32)
    m = (x - h).astype(jnp.bfloat16).astype(jnp.float32)
    return h, m, x - h - m


def splat(x, shape):
    return jnp.broadcast_to(x, shape)


def eliminate(ref):
    width = ref.shape[1]
    lanes = width // BS
    wide = lambda w: jnp.concatenate([w] * lanes, axis=1)
    for base in range(0, BS, 8):
        tile = ref[base : base + 8, :]
        rows = [splat(tile[i : i + 1, :], (8, width)) for i in range(8)]
        cols = [splat(tile[:, base + j : base + j + 1], (8, BS)) for j in range(8)]
        e = [[splat(cols[j][i : i + 1, :], (8, BS)) for j in range(i + 1)] for i in range(8)]
        for j in range(8):
            r = lax.rsqrt(e[j][j])
            rows[j] = rows[j] * wide(r)
            l = [None] * 8
            for i in range(j + 1, 8):
                l[i] = e[i][j] * r
            for i in range(j + 1, 8):
                for m in range(j + 1, i + 1):
                    e[i][m] = e[i][m] - l[i] * l[m]
                rows[i] = rows[i] - wide(l[i]) * rows[j]
        sub = lax.broadcasted_iota(jnp.int32, (8, width), 0)
        out = rows[0]
        for i in range(1, 8):
            out = jnp.where(sub == i, rows[i], out)
        below = lax.broadcasted_iota(jnp.int32, (8, BS), 0) + base
        upper = jnp.where(lax.broadcasted_iota(jnp.int32, (8, BS), 1) >= below, out[:, :BS], 0.0)
        out = jnp.concatenate([upper, out[:, BS:]], axis=1)
        ref[base : base + 8, :] = out
        if base + 8 < BS:
            h, m, l = split3(out)
            left = jnp.concatenate([w[:, :BS] for w in (h, h, m, m, h, l)], axis=0).astype(jnp.bfloat16)
            right = jnp.concatenate([h, m, h, m, l, h], axis=0).astype(jnp.bfloat16)
            d = lax.dot_general(left, right, (((0,), (0,)), ((), ())), preferred_element_type=jnp.float32)
            ref[base + 8 :, :] = ref[base + 8 :, :] - d[base + 8 :, :]


def factor_kernel(place, pair_ref, other_ref, wk_ref, corner_ref, one_ref, two_ref):
    row, col, k = place[0], place[1], place[2]
    rows = BS + 16

    def value(ref, base):
        s = ref[base + BS : base + rows, :].astype(jnp.float32)
        s = s[0:1] + s[1:2] + s[2:3]
        return ref[base : base + BS, :].astype(jnp.float32) * s

    def fill(core0, core1):
        one_ref[:, :BS] = value(core0, 0)
        one_ref[:, BS : 2 * BS] = value(core1, 0).T
        two_ref[:, :BS] = value(core1, rows)

    @pl.when(k == 0)
    def _():
        fill(pair_ref, other_ref)

    @pl.when(k == 1)
    def _():
        fill(other_ref, pair_ref)

    e = lax.broadcasted_iota(jnp.int32, (BS, BS), 0)
    f = lax.broadcasted_iota(jnp.int32, (BS, BS), 1)
    eye = jnp.where(e == f, 1.0, 0.0)
    one_ref[:, 2 * BS :] = eye
    eliminate(one_ref)
    l10t = one_ref[:, BS : 2 * BS].astype(jnp.bfloat16)
    w00 = one_ref[:, 2 * BS :]
    inner = (((0,), (0,)), ((), ()))
    two_ref[:, :BS] = two_ref[:, :BS] - lax.dot_general(l10t, l10t, inner, preferred_element_type=jnp.float32)
    two_ref[:, BS : 2 * BS] = eye
    parts = jnp.concatenate(split3(w00), axis=0).astype(jnp.bfloat16)
    two_ref[:, 2 * BS :] = -lax.dot_general(
        jnp.concatenate([l10t] * 3, axis=0), parts, inner, preferred_element_type=jnp.float32
    )
    eliminate(two_ref)

    def put(h, r, w):
        hi = w.astype(jnp.bfloat16)
        wk_ref[h, r * BS : (r + 1) * BS, :BS] = hi
        wk_ref[h, r * BS : (r + 1) * BS, BS:] = (w - hi.astype(jnp.float32)).astype(jnp.bfloat16)

    put(0, 0, w00)
    put(0, 1, two_ref[:, 2 * BS :])
    put(1, 0, jnp.zeros((BS, BS), jnp.float32))
    put(1, 1, two_ref[:, BS : 2 * BS])

    corner_ref[...] = l10t.astype(jnp.float32)

    @pl.when((row == 0) & (col == 0))
    def _():
        corner_ref[...] = one_ref[:, :BS].T

    @pl.when((row == 1) & (col == 0))
    def _():
        corner_ref[...] = l10t.astype(jnp.float32).T

    @pl.when((row == 1) & (col == 1))
    def _():
        corner_ref[...] = two_ref[:, :BS].T


def factor(place, pair, other):
    return pl.pallas_call(
        factor_kernel,
        grid_spec=pltpu.PrefetchScalarGridSpec(
            num_scalar_prefetch=1,
            in_specs=[pl.BlockSpec(memory_space=pltpu.VMEM)] * 2,
            out_specs=[pl.BlockSpec(memory_space=pltpu.VMEM)] * 2,
            scratch_shapes=[pltpu.VMEM((BS, 3 * BS), jnp.float32)] * 2,
        ),
        out_shape=[
            jax.ShapeDtypeStruct((2, 2 * BS, 2 * BS), jnp.bfloat16),
            jax.ShapeDtypeStruct((BS, BS), jnp.float32),
        ],
        compiler_params=pltpu.CompilerParams(vmem_limit_bytes=16 * 1024 * 1024),
        cost_estimate=pl.CostEstimate(flops=2 * 10**10, bytes_accessed=2**20, transcendentals=0),
        name="factor",
    )(place, pair, other)


def finish_kernel(place, a_ref, sc_ref, m0, m1, m2, m3, t0, t1, t2, t3, u_ref, v_ref, wk_ref, corner_ref,
                  out_ref, big_ref, q_ref, p_ref, prod_ref):
    step = pl.program_id(0)
    row, col, k, z, first = place[0], place[1], place[2], place[3], place[4]

    def scale_of(ref, base, a):
        s = ref[base + 4 * BS : base + 4 * BS + 16, :].astype(jnp.float32)
        return s[3 * a : 3 * a + 1] + s[3 * a + 1 : 3 * a + 2] + s[3 * a + 2 : 3 * a + 3]

    def panel_tiles(ref_m, ref_t, base, a0, wm, wt):
        def part(ref, w):
            raw = ref[base + a0 * BS : base + (a0 + 2) * BS, :]
            d = lax.dot_general(
                jnp.concatenate([raw, raw], axis=1), w, (((1,), (1,)), ((), ())), preferred_element_type=jnp.float32
            )
            out = []
            for a in range(2):
                s = scale_of(ref, base, a0 + a)
                out.append(d[a * BS : (a + 1) * BS] * jnp.concatenate([s, s], axis=1))
            return out

        return [(g + h).astype(jnp.bfloat16) for g, h in zip(part(ref_m, wm), part(ref_t, wt))]

    @pl.when(step == 0)
    def _():
        w_mine = wk_ref[k]
        w_other = wk_ref[1 - k]
        for i, (mine, other) in enumerate(((m0, t0), (m1, t1), (m2, t2), (m3, t3))):
            zs = lax.rem(z + (0, 3, 1, 2)[i], 4)
            for ys in range(2):
                for a0 in range(0, 4, 2):
                    tiles = panel_tiles(mine, other, ys * PIECE, a0, w_mine, w_other)
                    for a, tile in enumerate(tiles):
                        b = (a0 + a) * 8 + zs * 2 + ys
                        q_ref[pl.ds(pl.multiple_of(b * BS, BS), BS), :] = tile
        w_u = wk_ref[first]
        w_v = wk_ref[1 - first]
        for a0 in range(0, 4, 2):
            for a, tile in enumerate(panel_tiles(u_ref, v_ref, 0, a0, w_u, w_v)):
                p_ref[(a0 + a) * BS : (a0 + a + 1) * BS, :] = tile
        e = lax.broadcasted_iota(jnp.int32, (BS, 2 * BS), 0)
        f = lax.broadcasted_iota(jnp.int32, (BS, 2 * BS), 1)

        @pl.when(row < 2)
        def _():
            p_ref[0:BS, :] = jnp.where(f == e + row * BS, -1.0, 0.0).astype(jnp.bfloat16)

        @pl.when(col < 2)
        def _():
            q_ref[0:BS, :] = jnp.where(f == e + col * BS, -1.0, 0.0).astype(jnp.bfloat16)

    p = p_ref[pl.ds(pl.multiple_of(step * BS, BS), BS), :]
    for b in range(32):
        d = lax.dot_general(
            p, q_ref[b * BS : (b + 1) * BS, :], (((1,), (1,)), ((), ())), preferred_element_type=jnp.float32
        )
        prod_ref[pl.ds(b, BS, stride=40), :] = d

    @pl.when((step == 0) & (row < 2) & (col < 2))
    def _():
        prod_ref[pl.ds(0, BS, stride=40), :] = -corner_ref[...]

    sc = sc_ref[0]

    def update(e, mx):
        rows = pl.ds(pl.multiple_of(e * 40, 8), 32)
        m = a_ref[0, e].astype(jnp.float32) * sc - prod_ref[rows, :]
        prod_ref[rows, :] = m
        return jnp.maximum(mx, jnp.abs(m))

    mx = lax.fori_loop(0, BS, update, jnp.zeros((32, BS), jnp.float32), unroll=8)
    big = jnp.max(mx, axis=1, keepdims=True) + 1e-06
    big = jnp.broadcast_to(big, (32, BS))
    big_ref[0] = big.T[0:1]
    inv = 1.0 / big

    def divide(e, carry):
        rows = pl.ds(pl.multiple_of(e * 40, 8), 32)
        out_ref[0, e] = (prod_ref[rows, :] * inv).astype(jnp.bfloat16)
        return carry

    lax.fori_loop(0, BS, divide, 0, unroll=8)


def finish(place, blocks, sc, held, others, u, v, wk, corner):
    whole = lambda shape: pl.BlockSpec(memory_space=pltpu.VMEM)
    spec = pltpu.PrefetchScalarGridSpec(
        num_scalar_prefetch=1,
        grid=(4,),
        in_specs=[
            pl.BlockSpec((1, BS, 32, BS), lambda a, *_: (a, 0, 0, 0)),
            pl.BlockSpec((1, 32, BS), lambda a, *_: (a, 0, 0)),
        ]
        + [whole((2 * PIECE, BS))] * 8
        + [whole((PIECE, BS))] * 2
        + [whole((2, 2 * BS, 2 * BS)), whole((BS, BS))],
        out_specs=[
            pl.BlockSpec((1, BS, 32, BS), lambda a, *_: (a, 0, 0, 0)),
            pl.BlockSpec((1, 1, 32), lambda a, *_: (a, 0, 0)),
        ],
        scratch_shapes=[
            pltpu.VMEM((32 * BS, 2 * BS), jnp.bfloat16),
            pltpu.VMEM((4 * BS, 2 * BS), jnp.bfloat16),
            pltpu.VMEM((40 * BS, BS), jnp.float32),
        ],
    )
    return pl.pallas_call(
        finish_kernel,
        grid_spec=spec,
        out_shape=[
            jax.ShapeDtypeStruct((4, BS, 32, BS), jnp.bfloat16),
            jax.ShapeDtypeStruct((4, 1, 32), jnp.float32),
        ],
        compiler_params=pltpu.CompilerParams(vmem_limit_bytes=32 * 1024 * 1024),
        cost_estimate=pl.CostEstimate(flops=2 * 512 * 4096 * 512, bytes_accessed=12 * 2**20, transcendentals=0),
        name="finish",
    )(place, blocks, sc, *held, *others, u, v, wk, corner)


def on_device(blocks, scales):
    row = lax.axis_index("row")
    col = lax.axis_index("col")
    x = col
    k = row % 2
    y = (row // 2) % 4
    z = row // 8
    blocks = blocks.reshape(4, BS, 32, BS)
    scales = scales.reshape(4, 32)
    piece = strip(blocks, scales.reshape(4, 1, 32))
    first = jnp.where((x == 0) | (x == 3), 0, 1)
    place = jnp.stack([row, col, k, z, first]).astype(jnp.int32)
    u, v = along_x(piece, x)
    ours = jnp.where(first == k, u, v)
    mine = jnp.where(k == x % 2, ours, permute(jnp.where(first == k, v, u), sibling))
    head = lambda w: jnp.concatenate([w[:BS], w[4 * BS :]], axis=0)
    pair = jnp.concatenate([jnp.where(first == 0, head(u), head(v)), jnp.where(first == 0, head(v), head(u))], axis=0)
    pair, mine = lax.optimization_barrier((pair, mine))
    pair = lead_along(pair, y, 1)
    both = along_y(mine, y, x)
    pair = lead_along(pair, z, 0)
    pair, both = lax.optimization_barrier((pair, both))
    held = [both] + [permute(both, lambda z, y, k, x: (z + d, y, k, x)) for d in (1, -1, 2)]
    wk, corner = factor(place, pair, permute(pair, sibling))
    wk, *held[1:] = lax.optimization_barrier((wk, *held[1:]))
    others = [permute(h, sibling) for h in held]
    special = ((jnp.arange(4) == 0) & (row < 2))[:, None] | ((jnp.arange(32) == 0) & (col < 2))[None, :]
    sc = jnp.broadcast_to(jnp.where(special, 0.0, scales)[:, :, None], (4, 32, BS))
    factored, largest = finish(place, blocks, sc, held, others, u, v, wk, corner)
    return factored.reshape(4, 1, BS, 32, 1, BS), largest.reshape(4, 1, 32, 1)


def solution(mesh):
    in_specs = (P(None, "row", None, None, "col", None), P(None, "row", None, "col"))
    out_specs = (P(None, "row", None, None, "col", None), P(None, "row", None, "col"))
    return jax.shard_map(
        on_device, mesh=mesh, in_specs=in_specs, out_specs=out_specs, check_vma=False
    )
```

```python
import jax
import jax.numpy as jnp
from jax import lax
from jax.experimental import pallas as pl
from jax.experimental.pallas import tpu as pltpu
from jax.sharding import PartitionSpec as P

AXES = ("row", "col")
NX, NY, NZ, NK = 4, 4, 4, 2
BS = 128
PIECE = 4 * BS + 16


def dev(z, y, k, x):
    return (((z % NZ) * NY + (y % NY)) * NK + (k % NK)) * NX + (x % NX)


PLACES = [(z, y, k, x) for z in range(NZ) for y in range(NY) for k in range(NK) for x in range(NX)]


def permute(array, to):
    return lax.ppermute(array, AXES, [(dev(*place), dev(*to(*place))) for place in PLACES])


def sibling(z, y, k, x):
    return z, y, 1 - k, x


def strip_kernel(blocks_ref, scales_ref, piece_ref):
    sub = lax.broadcasted_iota(jnp.int32, (16, BS), 0)
    rows = jnp.zeros((16, BS), jnp.float32)
    for a in range(4):
        for t, part in enumerate(split3(jnp.broadcast_to(scales_ref[a, 0:1, 0:1], (16, BS)))):
            rows = jnp.where(sub == 3 * a + t, part, rows)
    rows = rows.astype(jnp.bfloat16)
    for a in range(4):
        piece_ref[a * BS : (a + 1) * BS, :] = blocks_ref[a, :, 0, :]
    piece_ref[4 * BS :, :] = rows


def strip(blocks, scales):
    return pl.pallas_call(
        strip_kernel,
        grid=(1,),
        in_specs=[
            pl.BlockSpec((4, BS, 16, BS), lambda i: (0, 0, 0, 0)),
            pl.BlockSpec((4, 1, 32), lambda i: (0, 0, 0)),
        ],
        out_specs=pl.BlockSpec((PIECE, BS), lambda i: (0, 0)),
        out_shape=jax.ShapeDtypeStruct((PIECE, BS), jnp.bfloat16),
        compiler_params=pltpu.CompilerParams(vmem_limit_bytes=60 * 1024 * 1024),
        cost_estimate=pl.CostEstimate(flops=0, bytes_accessed=2 * 2**20, transcendentals=0),
        name="strip",
    )(blocks, scales)


def along_x(array, x):
    got = [
        permute(array, lambda z, y, k, x: (z, y, k, hop[x])) for hop in ((1, 0, 3, 2), (3, 2, 1, 0), (2, 3, 0, 1))
    ]
    return got


def by_column(array, got, x):
    u = jnp.where(x <= 1, array, got[1])
    v = jnp.where(x <= 1, got[0], got[2])
    return u, v


def trade(p, q):
    return (q if p == 0 else 0), p in (0, q)


def pick(at, zero, one, two, three):
    return jnp.where(at == 0, zero, jnp.where(at == 1, one, jnp.where(at == 2, two, three)))


def along_y(mine, y, x):
    def across(z, y, k, x):
        return (z, y + 2, k, x) if y % 2 == x // 2 else (z, y, 1 - k, x)

    up = permute(mine, lambda z, y, k, x: (z, y + 1, k, x))
    down = permute(mine, lambda z, y, k, x: (z, y - 1, k, x))
    over = permute(mine, across)
    turn = (y - x // 2) % 4
    slots = [pick(turn, mine, up, over, down), pick(turn, over, down, mine, up)]
    return jnp.concatenate(slots, axis=0)


def lead_along(pair, at, axis):
    got = []
    for q in (1, 2, 3):

        def place(*here):
            there = list(here)
            other, moves = trade(here[axis], q)
            there[axis if moves else 2] = other if moves else 1 - here[2]
            return there

        got.append(permute(pair, place))
    return pick(at, pair, *got)


def split3(x):
    h = x.astype(jnp.bfloat16).astype(jnp.float32)
    m = (x - h).astype(jnp.bfloat16).astype(jnp.float32)
    return h, m, x - h - m


def splat(x, shape):
    return jnp.broadcast_to(x, shape)


def eliminate(ref):
    width = ref.shape[1]
    lanes = width // BS
    wide = lambda w: jnp.concatenate([w] * lanes, axis=1)
    for base in range(0, BS, 16):
        tile = ref[base : base + 16, :]
        rows = [splat(tile[i : i + 1, :], (8, width)) for i in range(16)]
        cols = [splat(tile[:, base + j : base + j + 1], (16, BS)) for j in range(16)]
        e = [[splat(cols[j][i : i + 1, :], (8, BS)) for j in range(i + 1)] for i in range(16)]
        for j in range(16):
            r = lax.rsqrt(e[j][j])
            rows[j] = rows[j] * wide(r)
            l = [None] * 16
            for i in range(j + 1, 16):
                l[i] = e[i][j] * r
            for i in range(j + 1, 16):
                for m in range(j + 1, i + 1):
                    e[i][m] = e[i][m] - l[i] * l[m]
                rows[i] = rows[i] - wide(l[i]) * rows[j]
        sub = lax.broadcasted_iota(jnp.int32, (8, width), 0)
        out = []
        for g in range(0, 16, 8):
            acc = rows[g]
            for i in range(1, 8):
                acc = jnp.where(sub == i, rows[g + i], acc)
            out.append(acc)
        out = jnp.concatenate(out, axis=0)
        below = lax.broadcasted_iota(jnp.int32, (16, BS), 0) + base
        upper = jnp.where(lax.broadcasted_iota(jnp.int32, (16, BS), 1) >= below, out[:, :BS], 0.0)
        out = jnp.concatenate([upper, out[:, BS:]], axis=1)
        ref[base : base + 16, :] = out
        if base + 16 < BS:
            h, m, l = split3(out)
            left = jnp.concatenate([w[:, :BS] for w in (h, h, m, m, h, l)], axis=0).astype(jnp.bfloat16)
            right = jnp.concatenate([h, m, h, m, l, h], axis=0).astype(jnp.bfloat16)
            d = lax.dot_general(left, right, (((0,), (0,)), ((), ())), preferred_element_type=jnp.float32)
            ref[base + 16 :, :] = ref[base + 16 :, :] - d[base + 16 :, :]


def factor_kernel(place, pair_ref, other_ref, wk_ref, corner_ref, one_ref, two_ref):
    row, col, k = place[0], place[1], place[2]
    rows = BS + 16

    def value(ref, base):
        s = ref[base + BS : base + rows, :].astype(jnp.float32)
        s = s[0:1] + s[1:2] + s[2:3]
        return ref[base : base + BS, :].astype(jnp.float32) * s

    def fill(core0, core1):
        one_ref[:, :BS] = value(core0, 0)
        one_ref[:, BS : 2 * BS] = value(core1, 0).T
        two_ref[:, :BS] = value(core1, rows)

    @pl.when(k == 0)
    def _():
        fill(pair_ref, other_ref)

    @pl.when(k == 1)
    def _():
        fill(other_ref, pair_ref)

    e = lax.broadcasted_iota(jnp.int32, (BS, BS), 0)
    f = lax.broadcasted_iota(jnp.int32, (BS, BS), 1)
    eye = jnp.where(e == f, 1.0, 0.0)
    one_ref[:, 2 * BS :] = eye
    eliminate(one_ref)
    l10t = one_ref[:, BS : 2 * BS].astype(jnp.bfloat16)
    w00 = one_ref[:, 2 * BS :]
    inner = (((0,), (0,)), ((), ()))
    two_ref[:, :BS] = two_ref[:, :BS] - lax.dot_general(l10t, l10t, inner, preferred_element_type=jnp.float32)
    two_ref[:, BS : 2 * BS] = eye
    parts = jnp.concatenate(split3(w00), axis=0).astype(jnp.bfloat16)
    two_ref[:, 2 * BS :] = -lax.dot_general(
        jnp.concatenate([l10t] * 3, axis=0), parts, inner, preferred_element_type=jnp.float32
    )
    eliminate(two_ref)

    def put(h, r, w):
        hi = w.astype(jnp.bfloat16)
        wk_ref[h, r * BS : (r + 1) * BS, :BS] = hi
        wk_ref[h, r * BS : (r + 1) * BS, BS:] = (w - hi.astype(jnp.float32)).astype(jnp.bfloat16)

    put(0, 0, w00)
    put(0, 1, two_ref[:, 2 * BS :])
    put(1, 0, jnp.zeros((BS, BS), jnp.float32))
    put(1, 1, two_ref[:, BS : 2 * BS])

    corner_ref[...] = l10t.astype(jnp.float32)

    @pl.when((row == 0) & (col == 0))
    def _():
        corner_ref[...] = one_ref[:, :BS].T

    @pl.when((row == 1) & (col == 0))
    def _():
        corner_ref[...] = l10t.astype(jnp.float32).T

    @pl.when((row == 1) & (col == 1))
    def _():
        corner_ref[...] = two_ref[:, :BS].T


def factor(place, pair, other):
    return pl.pallas_call(
        factor_kernel,
        grid_spec=pltpu.PrefetchScalarGridSpec(
            num_scalar_prefetch=1,
            in_specs=[pl.BlockSpec(memory_space=pltpu.VMEM)] * 2,
            out_specs=[pl.BlockSpec(memory_space=pltpu.VMEM)] * 2,
            scratch_shapes=[pltpu.VMEM((BS, 3 * BS), jnp.float32)] * 2,
        ),
        out_shape=[
            jax.ShapeDtypeStruct((2, 2 * BS, 2 * BS), jnp.bfloat16),
            jax.ShapeDtypeStruct((BS, BS), jnp.float32),
        ],
        compiler_params=pltpu.CompilerParams(vmem_limit_bytes=16 * 1024 * 1024),
        cost_estimate=pl.CostEstimate(flops=10**6, bytes_accessed=2**16, transcendentals=0),
        name="factor",
    )(place, pair, other)


def finish_kernel(place, a_ref, sc_ref, m0, m1, m2, m3, t0, t1, t2, t3, u_ref, v_ref, wk_ref, corner_ref,
                  out_ref, big_ref, q_ref, p_ref, prod_ref):
    step = pl.program_id(0)
    row, col, k, z, first = place[0], place[1], place[2], place[3], place[4]

    def scale_of(ref, base, a):
        s = ref[base + 4 * BS : base + 4 * BS + 16, :].astype(jnp.float32)
        return s[3 * a : 3 * a + 1] + s[3 * a + 1 : 3 * a + 2] + s[3 * a + 2 : 3 * a + 3]

    def panel_tiles(ref_m, ref_t, base, a0, wm, wt):
        def part(ref, w):
            raw = ref[base + a0 * BS : base + (a0 + 2) * BS, :]
            d = lax.dot_general(
                jnp.concatenate([raw, raw], axis=1), w, (((1,), (1,)), ((), ())), preferred_element_type=jnp.float32
            )
            out = []
            for a in range(2):
                s = scale_of(ref, base, a0 + a)
                out.append(d[a * BS : (a + 1) * BS] * jnp.concatenate([s, s], axis=1))
            return out

        return [(g + h).astype(jnp.bfloat16) for g, h in zip(part(ref_m, wm), part(ref_t, wt))]

    @pl.when(step == 0)
    def _():
        w_mine = wk_ref[k]
        w_other = wk_ref[1 - k]
        for i, (mine, other) in enumerate(((m0, t0), (m1, t1), (m2, t2), (m3, t3))):
            zs = lax.rem(z + (0, 3, 1, 2)[i], 4)
            for ys in range(2):
                for a0 in range(0, 4, 2):
                    tiles = panel_tiles(mine, other, ys * PIECE, a0, w_mine, w_other)
                    for a, tile in enumerate(tiles):
                        b = (a0 + a) * 8 + zs * 2 + ys
                        q_ref[pl.ds(pl.multiple_of(b * BS, BS), BS), :] = tile
        w_u = wk_ref[first]
        w_v = wk_ref[1 - first]
        for a0 in range(0, 4, 2):
            for a, tile in enumerate(panel_tiles(u_ref, v_ref, 0, a0, w_u, w_v)):
                p_ref[(a0 + a) * BS : (a0 + a + 1) * BS, :] = tile
        e = lax.broadcasted_iota(jnp.int32, (BS, 2 * BS), 0)
        f = lax.broadcasted_iota(jnp.int32, (BS, 2 * BS), 1)

        @pl.when(row < 2)
        def _():
            p_ref[0:BS, :] = jnp.where(f == e + row * BS, -1.0, 0.0).astype(jnp.bfloat16)

        @pl.when(col < 2)
        def _():
            q_ref[0:BS, :] = jnp.where(f == e + col * BS, -1.0, 0.0).astype(jnp.bfloat16)

    p = p_ref[pl.ds(pl.multiple_of(step * BS, BS), BS), :]
    for b in range(32):
        d = lax.dot_general(
            p, q_ref[b * BS : (b + 1) * BS, :], (((1,), (1,)), ((), ())), preferred_element_type=jnp.float32
        )
        prod_ref[pl.ds(b, BS, stride=40), :] = d

    @pl.when((step == 0) & (row < 2) & (col < 2))
    def _():
        prod_ref[pl.ds(0, BS, stride=40), :] = -corner_ref[...]

    sc = sc_ref[0]

    def update(e, mx):
        rows = pl.ds(pl.multiple_of(e * 40, 8), 32)
        m = a_ref[0, e].astype(jnp.float32) * sc - prod_ref[rows, :]
        prod_ref[rows, :] = m
        return jnp.maximum(mx, jnp.abs(m))

    mx = lax.fori_loop(0, BS, update, jnp.zeros((32, BS), jnp.float32), unroll=8)
    big = jnp.max(mx, axis=1, keepdims=True) + 1e-06
    big = jnp.broadcast_to(big, (32, BS))
    big_ref[0] = big.T[0:1]
    inv = 1.0 / big

    def divide(e, carry):
        rows = pl.ds(pl.multiple_of(e * 40, 8), 32)
        out_ref[0, e] = (prod_ref[rows, :] * inv).astype(jnp.bfloat16)
        return carry

    lax.fori_loop(0, BS, divide, 0, unroll=8)


def finish(place, blocks, sc, held, others, u, v, wk, corner):
    whole = lambda shape: pl.BlockSpec(memory_space=pltpu.VMEM)
    spec = pltpu.PrefetchScalarGridSpec(
        num_scalar_prefetch=1,
        grid=(4,),
        in_specs=[
            pl.BlockSpec((1, BS, 32, BS), lambda a, *_: (a, 0, 0, 0)),
            pl.BlockSpec((1, 32, BS), lambda a, *_: (a, 0, 0)),
        ]
        + [whole((2 * PIECE, BS))] * 8
        + [whole((PIECE, BS))] * 2
        + [whole((2, 2 * BS, 2 * BS)), whole((BS, BS))],
        out_specs=[
            pl.BlockSpec((1, BS, 32, BS), lambda a, *_: (a, 0, 0, 0)),
            pl.BlockSpec((1, 1, 32), lambda a, *_: (a, 0, 0)),
        ],
        scratch_shapes=[
            pltpu.VMEM((32 * BS, 2 * BS), jnp.bfloat16),
            pltpu.VMEM((4 * BS, 2 * BS), jnp.bfloat16),
            pltpu.VMEM((40 * BS, BS), jnp.float32),
        ],
    )
    return pl.pallas_call(
        finish_kernel,
        grid_spec=spec,
        out_shape=[
            jax.ShapeDtypeStruct((4, BS, 32, BS), jnp.bfloat16),
            jax.ShapeDtypeStruct((4, 1, 32), jnp.float32),
        ],
        compiler_params=pltpu.CompilerParams(vmem_limit_bytes=32 * 1024 * 1024),
        cost_estimate=pl.CostEstimate(flops=2 * 512 * 4096 * 512, bytes_accessed=12 * 2**20, transcendentals=0),
        name="finish",
    )(place, blocks, sc, *held, *others, u, v, wk, corner)


def on_device(blocks, scales):
    row = lax.axis_index("row")
    col = lax.axis_index("col")
    x = col
    k = row % 2
    y = (row // 2) % 4
    z = row // 8
    blocks = blocks.reshape(4, BS, 32, BS)
    scales = scales.reshape(4, 32)
    piece = strip(blocks, scales.reshape(4, 1, 32))
    first = jnp.where((x == 0) | (x == 3), 0, 1)
    place = jnp.stack([row, col, k, z, first]).astype(jnp.int32)
    got = along_x(piece, x)
    u, v = by_column(piece, got, x)
    ours = jnp.where(first == k, u, v)
    mine = jnp.where(k == x % 2, ours, permute(jnp.where(first == k, v, u), sibling))
    head = lambda w: jnp.concatenate([w[:BS], w[4 * BS :]], axis=0)
    pair = jnp.concatenate([jnp.where(first == 0, head(u), head(v)), jnp.where(first == 0, head(v), head(u))], axis=0)
    pair, mine = lax.optimization_barrier((pair, mine))
    pair = lead_along(pair, y, 1)
    both = along_y(mine, y, x)
    pair = lead_along(pair, z, 0)
    pair, piece, got = lax.optimization_barrier((pair, piece, got))
    u, v = by_column(piece, got, x)
    held = [both] + [permute(both, lambda z, y, k, x: (z + d, y, k, x)) for d in (1, -1, 2)]
    wk, corner = factor(place, pair, permute(pair, sibling))
    wk, *held[1:] = lax.optimization_barrier((wk, *held[1:]))
    others = [permute(h, sibling) for h in held]
    special = ((jnp.arange(4) == 0) & (row < 2))[:, None] | ((jnp.arange(32) == 0) & (col < 2))[None, :]
    sc = jnp.broadcast_to(jnp.where(special, 0.0, scales)[:, :, None], (4, 32, BS))
    factored, largest = finish(place, blocks, sc, held, others, u, v, wk, corner)
    return factored.reshape(4, 1, BS, 32, 1, BS), largest.reshape(4, 1, 32, 1)


def solution(mesh):
    in_specs = (P(None, "row", None, None, "col", None), P(None, "row", None, "col"))
    out_specs = (P(None, "row", None, None, "col", None), P(None, "row", None, "col"))
    return jax.shard_map(
        on_device, mesh=mesh, in_specs=in_specs, out_specs=out_specs, check_vma=False
    )
```

```python
import jax
import jax.numpy as jnp
from jax import lax
from jax.experimental import pallas as pl
from jax.experimental.pallas import tpu as pltpu
from jax.sharding import PartitionSpec as P

AXES = ("row", "col")
NX, NY, NZ, NK = 4, 4, 4, 2
BS = 128
PIECE = 4 * BS + 16


def dev(z, y, k, x):
    return (((z % NZ) * NY + (y % NY)) * NK + (k % NK)) * NX + (x % NX)


PLACES = [(z, y, k, x) for z in range(NZ) for y in range(NY) for k in range(NK) for x in range(NX)]


def permute(array, to):
    return lax.ppermute(array, AXES, [(dev(*place), dev(*to(*place))) for place in PLACES])


def sibling(z, y, k, x):
    return z, y, 1 - k, x


def strip_kernel(blocks_ref, scales_ref, piece_ref):
    sub = lax.broadcasted_iota(jnp.int32, (16, BS), 0)
    rows = jnp.zeros((16, BS), jnp.float32)
    for a in range(4):
        for t, part in enumerate(split3(jnp.broadcast_to(scales_ref[a, 0:1, 0:1], (16, BS)))):
            rows = jnp.where(sub == 3 * a + t, part, rows)
    rows = rows.astype(jnp.bfloat16)
    for a in range(4):
        piece_ref[a * BS : (a + 1) * BS, :] = blocks_ref[a, :, 0, :]
    piece_ref[4 * BS :, :] = rows


def strip(blocks, scales):
    return pl.pallas_call(
        strip_kernel,
        grid=(1,),
        in_specs=[
            pl.BlockSpec((4, BS, 16, BS), lambda i: (0, 0, 0, 0)),
            pl.BlockSpec((4, 1, 32), lambda i: (0, 0, 0)),
        ],
        out_specs=pl.BlockSpec((PIECE, BS), lambda i: (0, 0)),
        out_shape=jax.ShapeDtypeStruct((PIECE, BS), jnp.bfloat16),
        compiler_params=pltpu.CompilerParams(vmem_limit_bytes=60 * 1024 * 1024),
        cost_estimate=pl.CostEstimate(flops=0, bytes_accessed=2 * 2**20, transcendentals=0),
        name="strip",
    )(blocks, scales)


def along_x(array, x):
    got = [
        permute(array, lambda z, y, k, x: (z, y, k, hop[x])) for hop in ((1, 0, 3, 2), (3, 2, 1, 0), (2, 3, 0, 1))
    ]
    return got


def by_column(array, got, x):
    u = jnp.where(x <= 1, array, got[1])
    v = jnp.where(x <= 1, got[0], got[2])
    return u, v


def trade(p, q):
    return (q if p == 0 else 0), p in (0, q)


def pick(at, zero, one, two, three):
    return jnp.where(at == 0, zero, jnp.where(at == 1, one, jnp.where(at == 2, two, three)))


def along_y(mine, y, x):
    def across(z, y, k, x):
        return (z, y + 2, k, x) if y % 2 == x // 2 else (z, y, 1 - k, x)

    up = permute(mine, lambda z, y, k, x: (z, y + 1, k, x))
    down = permute(mine, lambda z, y, k, x: (z, y - 1, k, x))
    over = permute(mine, across)
    turn = (y - x // 2) % 4
    slots = [pick(turn, mine, up, over, down), pick(turn, over, down, mine, up)]
    return jnp.concatenate(slots, axis=0)


def lead_along(pair, at, axis):
    got = []
    for q in (1, 2, 3):

        def place(*here):
            there = list(here)
            other, moves = trade(here[axis], q)
            there[axis if moves else 2] = other if moves else 1 - here[2]
            return there

        got.append(permute(pair, place))
    return pick(at, pair, *got)


def split3(x):
    h = x.astype(jnp.bfloat16).astype(jnp.float32)
    m = (x - h).astype(jnp.bfloat16).astype(jnp.float32)
    return h, m, x - h - m


def splat(x, shape):
    return jnp.broadcast_to(x, shape)


def eliminate(ref):
    width = ref.shape[1]
    lanes = width // BS
    wide = lambda w: jnp.concatenate([w] * lanes, axis=1)
    for base in range(0, BS, 16):
        tile = ref[base : base + 16, :]
        rows = [splat(tile[i : i + 1, :], (8, width)) for i in range(16)]
        cols = [splat(tile[:, base + j : base + j + 1], (16, BS)) for j in range(16)]
        e = [[splat(cols[j][i : i + 1, :], (8, BS)) for j in range(i + 1)] for i in range(16)]
        for j in range(16):
            r = lax.rsqrt(e[j][j])
            rows[j] = rows[j] * wide(r)
            l = [None] * 16
            for i in range(j + 1, 16):
                l[i] = e[i][j] * r
            for i in range(j + 1, 16):
                for m in range(j + 1, i + 1):
                    e[i][m] = e[i][m] - l[i] * l[m]
                rows[i] = rows[i] - wide(l[i]) * rows[j]
        sub = lax.broadcasted_iota(jnp.int32, (8, width), 0)
        out = []
        for g in range(0, 16, 8):
            acc = rows[g]
            for i in range(1, 8):
                acc = jnp.where(sub == i, rows[g + i], acc)
            out.append(acc)
        out = jnp.concatenate(out, axis=0)
        below = lax.broadcasted_iota(jnp.int32, (16, BS), 0) + base
        upper = jnp.where(lax.broadcasted_iota(jnp.int32, (16, BS), 1) >= below, out[:, :BS], 0.0)
        out = jnp.concatenate([upper, out[:, BS:]], axis=1)
        ref[base : base + 16, :] = out
        if base + 16 < BS:
            h, m, l = split3(out)
            left = jnp.concatenate([w[:, :BS] for w in (h, h, m, m, h, l)], axis=0).astype(jnp.bfloat16)
            right = jnp.concatenate([h, m, h, m, l, h], axis=0).astype(jnp.bfloat16)
            d = lax.dot_general(left, right, (((0,), (0,)), ((), ())), preferred_element_type=jnp.float32)
            ref[base + 16 :, :] = ref[base + 16 :, :] - d[base + 16 :, :]


def factor_kernel(place, pair_ref, other_ref, wk_ref, corner_ref, one_ref, two_ref):
    row, col, k = place[0], place[1], place[2]
    rows = BS + 16

    def value(ref, base):
        s = ref[base + BS : base + rows, :].astype(jnp.float32)
        s = s[0:1] + s[1:2] + s[2:3]
        return ref[base : base + BS, :].astype(jnp.float32) * s

    def fill(core0, core1):
        one_ref[:, :BS] = value(core0, 0)
        one_ref[:, BS : 2 * BS] = value(core1, 0).T
        two_ref[:, :BS] = value(core1, rows)

    @pl.when(k == 0)
    def _():
        fill(pair_ref, other_ref)

    @pl.when(k == 1)
    def _():
        fill(other_ref, pair_ref)

    e = lax.broadcasted_iota(jnp.int32, (BS, BS), 0)
    f = lax.broadcasted_iota(jnp.int32, (BS, BS), 1)
    eye = jnp.where(e == f, 1.0, 0.0)
    one_ref[:, 2 * BS :] = eye
    eliminate(one_ref)
    l10t = one_ref[:, BS : 2 * BS].astype(jnp.bfloat16)
    w00 = one_ref[:, 2 * BS :]
    inner = (((0,), (0,)), ((), ()))
    two_ref[:, :BS] = two_ref[:, :BS] - lax.dot_general(l10t, l10t, inner, preferred_element_type=jnp.float32)
    two_ref[:, BS : 2 * BS] = eye
    parts = jnp.concatenate(split3(w00), axis=0).astype(jnp.bfloat16)
    two_ref[:, 2 * BS :] = -lax.dot_general(
        jnp.concatenate([l10t] * 3, axis=0), parts, inner, preferred_element_type=jnp.float32
    )
    eliminate(two_ref)

    def put(h, r, w):
        hi = w.astype(jnp.bfloat16)
        wk_ref[h, r * BS : (r + 1) * BS, :BS] = hi
        wk_ref[h, r * BS : (r + 1) * BS, BS:] = (w - hi.astype(jnp.float32)).astype(jnp.bfloat16)

    put(0, 0, w00)
    put(0, 1, two_ref[:, 2 * BS :])
    put(1, 0, jnp.zeros((BS, BS), jnp.float32))
    put(1, 1, two_ref[:, BS : 2 * BS])

    corner_ref[...] = l10t.astype(jnp.float32)

    @pl.when((row == 0) & (col == 0))
    def _():
        corner_ref[...] = one_ref[:, :BS].T

    @pl.when((row == 1) & (col == 0))
    def _():
        corner_ref[...] = l10t.astype(jnp.float32).T

    @pl.when((row == 1) & (col == 1))
    def _():
        corner_ref[...] = two_ref[:, :BS].T


def factor(place, pair, other):
    return pl.pallas_call(
        factor_kernel,
        grid_spec=pltpu.PrefetchScalarGridSpec(
            num_scalar_prefetch=1,
            in_specs=[pl.BlockSpec(memory_space=pltpu.VMEM)] * 2,
            out_specs=[pl.BlockSpec(memory_space=pltpu.VMEM)] * 2,
            scratch_shapes=[pltpu.VMEM((BS, 3 * BS), jnp.float32)] * 2,
        ),
        out_shape=[
            jax.ShapeDtypeStruct((2, 2 * BS, 2 * BS), jnp.bfloat16),
            jax.ShapeDtypeStruct((BS, BS), jnp.float32),
        ],
        compiler_params=pltpu.CompilerParams(vmem_limit_bytes=16 * 1024 * 1024),
        cost_estimate=pl.CostEstimate(flops=10**6, bytes_accessed=2**16, transcendentals=0),
        name="factor",
    )(place, pair, other)


def finish_kernel(place, a_ref, sc_ref, m0, m1, m2, m3, t0, t1, t2, t3, u_ref, v_ref, wk_ref, corner_ref,
                  out_ref, big_ref, q_ref, p_ref, prod_ref):
    step = pl.program_id(0)
    row, col, k, z, first = place[0], place[1], place[2], place[3], place[4]

    def scale_of(ref, base, a):
        s = ref[base + 4 * BS : base + 4 * BS + 16, :].astype(jnp.float32)
        return s[3 * a : 3 * a + 1] + s[3 * a + 1 : 3 * a + 2] + s[3 * a + 2 : 3 * a + 3]

    def panel_tiles(ref_m, ref_t, base, a0, wm, wt):
        def part(ref, w):
            raw = ref[base + a0 * BS : base + (a0 + 2) * BS, :]
            d = lax.dot_general(
                jnp.concatenate([raw, raw], axis=1), w, (((1,), (1,)), ((), ())), preferred_element_type=jnp.float32
            )
            out = []
            for a in range(2):
                s = scale_of(ref, base, a0 + a)
                out.append(d[a * BS : (a + 1) * BS] * jnp.concatenate([s, s], axis=1))
            return out

        return [(g + h).astype(jnp.bfloat16) for g, h in zip(part(ref_m, wm), part(ref_t, wt))]

    @pl.when(step == 0)
    def _():
        w_mine = wk_ref[k]
        w_other = wk_ref[1 - k]
        for i, (mine, other) in enumerate(((m0, t0), (m1, t1), (m2, t2), (m3, t3))):
            zs = lax.rem(z + (0, 3, 1, 2)[i], 4)
            for ys in range(2):
                for a0 in range(0, 4, 2):
                    tiles = panel_tiles(mine, other, ys * PIECE, a0, w_mine, w_other)
                    for a, tile in enumerate(tiles):
                        b = (a0 + a) * 8 + zs * 2 + ys
                        q_ref[pl.ds(pl.multiple_of(b * BS, BS), BS), :] = tile
        w_u = wk_ref[first]
        w_v = wk_ref[1 - first]
        for a0 in range(0, 4, 2):
            for a, tile in enumerate(panel_tiles(u_ref, v_ref, 0, a0, w_u, w_v)):
                p_ref[(a0 + a) * BS : (a0 + a + 1) * BS, :] = tile
        e = lax.broadcasted_iota(jnp.int32, (BS, 2 * BS), 0)
        f = lax.broadcasted_iota(jnp.int32, (BS, 2 * BS), 1)

        @pl.when(row < 2)
        def _():
            p_ref[0:BS, :] = jnp.where(f == e + row * BS, -1.0, 0.0).astype(jnp.bfloat16)

        @pl.when(col < 2)
        def _():
            q_ref[0:BS, :] = jnp.where(f == e + col * BS, -1.0, 0.0).astype(jnp.bfloat16)

    p = p_ref[pl.ds(pl.multiple_of(step * BS, BS), BS), :]
    for b in range(32):
        d = lax.dot_general(
            p, q_ref[b * BS : (b + 1) * BS, :], (((1,), (1,)), ((), ())), preferred_element_type=jnp.float32
        )
        prod_ref[pl.ds(b, BS, stride=40), :] = d

    @pl.when((step == 0) & (row < 2) & (col < 2))
    def _():
        prod_ref[pl.ds(0, BS, stride=40), :] = -corner_ref[...]

    sc = sc_ref[0]

    def update(e, mx):
        rows = pl.ds(pl.multiple_of(e * 40, 8), 32)
        m = a_ref[0, e].astype(jnp.float32) * sc - prod_ref[rows, :]
        prod_ref[rows, :] = m
        return jnp.maximum(mx, jnp.abs(m))

    mx = lax.fori_loop(0, BS, update, jnp.zeros((32, BS), jnp.float32), unroll=8)
    big = jnp.max(mx, axis=1, keepdims=True) + 1e-06
    big = jnp.broadcast_to(big, (32, BS))
    big_ref[0] = big.T[0:1]
    inv = 1.0 / big

    def divide(e, carry):
        rows = pl.ds(pl.multiple_of(e * 40, 8), 32)
        out_ref[0, e] = (prod_ref[rows, :] * inv).astype(jnp.bfloat16)
        return carry

    lax.fori_loop(0, BS, divide, 0, unroll=8)


def finish(place, blocks, sc, held, others, u, v, wk, corner):
    whole = lambda shape: pl.BlockSpec(memory_space=pltpu.VMEM)
    spec = pltpu.PrefetchScalarGridSpec(
        num_scalar_prefetch=1,
        grid=(4,),
        in_specs=[
            pl.BlockSpec((1, BS, 32, BS), lambda a, *_: (a, 0, 0, 0)),
            pl.BlockSpec((1, 32, BS), lambda a, *_: (a, 0, 0)),
        ]
        + [whole((2 * PIECE, BS))] * 8
        + [whole((PIECE, BS))] * 2
        + [whole((2, 2 * BS, 2 * BS)), whole((BS, BS))],
        out_specs=[
            pl.BlockSpec((1, BS, 32, BS), lambda a, *_: (a, 0, 0, 0)),
            pl.BlockSpec((1, 1, 32), lambda a, *_: (a, 0, 0)),
        ],
        scratch_shapes=[
            pltpu.VMEM((32 * BS, 2 * BS), jnp.bfloat16),
            pltpu.VMEM((4 * BS, 2 * BS), jnp.bfloat16),
            pltpu.VMEM((40 * BS, BS), jnp.float32),
        ],
    )
    return pl.pallas_call(
        finish_kernel,
        grid_spec=spec,
        out_shape=[
            jax.ShapeDtypeStruct((4, BS, 32, BS), jnp.bfloat16),
            jax.ShapeDtypeStruct((4, 1, 32), jnp.float32),
        ],
        compiler_params=pltpu.CompilerParams(vmem_limit_bytes=32 * 1024 * 1024),
        cost_estimate=pl.CostEstimate(flops=2 * 512 * 4096 * 512, bytes_accessed=12 * 2**20, transcendentals=0),
        name="finish",
    )(place, blocks, sc, *held, *others, u, v, wk, corner)


def on_device(blocks, scales):
    row = lax.axis_index("row")
    col = lax.axis_index("col")
    x = col
    k = row % 2
    y = (row // 2) % 4
    z = row // 8
    blocks = blocks.reshape(4, BS, 32, BS)
    scales = scales.reshape(4, 32)
    piece = strip(blocks, scales.reshape(4, 1, 32))
    first = jnp.where((x == 0) | (x == 3), 0, 1)
    place = jnp.stack([row, col, k, z, first]).astype(jnp.int32)
    got = along_x(piece, x)
    u, v = by_column(piece, got, x)
    ours = jnp.where(first == k, u, v)
    mine = jnp.where(k == x % 2, ours, permute(jnp.where(first == k, v, u), sibling))
    head = lambda w: jnp.concatenate([w[:BS], w[4 * BS :]], axis=0)
    pair = jnp.concatenate([jnp.where(first == 0, head(u), head(v)), jnp.where(first == 0, head(v), head(u))], axis=0)
    pair = lead_along(pair, y, 1)
    both = along_y(mine, y, x)
    pair = lead_along(pair, z, 0)
    pair, piece, got = lax.optimization_barrier((pair, piece, got))
    u, v = by_column(piece, got, x)
    held = [both] + [permute(both, lambda z, y, k, x: (z + d, y, k, x)) for d in (1, -1, 2)]
    wk, corner = factor(place, pair, permute(pair, sibling))
    wk, *held[1:] = lax.optimization_barrier((wk, *held[1:]))
    others = [permute(h, sibling) for h in held]
    special = ((jnp.arange(4) == 0) & (row < 2))[:, None] | ((jnp.arange(32) == 0) & (col < 2))[None, :]
    sc = jnp.broadcast_to(jnp.where(special, 0.0, scales)[:, :, None], (4, 32, BS))
    factored, largest = finish(place, blocks, sc, held, others, u, v, wk, corner)
    return factored.reshape(4, 1, BS, 32, 1, BS), largest.reshape(4, 1, 32, 1)


def solution(mesh):
    in_specs = (P(None, "row", None, None, "col", None), P(None, "row", None, "col"))
    out_specs = (P(None, "row", None, None, "col", None), P(None, "row", None, "col"))
    return jax.shard_map(
        on_device, mesh=mesh, in_specs=in_specs, out_specs=out_specs, check_vma=False
    )
```

```python
import jax
import jax.numpy as jnp
from jax import lax
from jax.experimental import pallas as pl
from jax.experimental.pallas import tpu as pltpu
from jax.sharding import PartitionSpec as P

AXES = ("row", "col")
NX, NY, NZ, NK = 4, 4, 4, 2
BS = 128
PIECE = 4 * BS + 16


def dev(z, y, k, x):
    return (((z % NZ) * NY + (y % NY)) * NK + (k % NK)) * NX + (x % NX)


PLACES = [(z, y, k, x) for z in range(NZ) for y in range(NY) for k in range(NK) for x in range(NX)]


def permute(array, to):
    return lax.ppermute(array, AXES, [(dev(*place), dev(*to(*place))) for place in PLACES])


def sibling(z, y, k, x):
    return z, y, 1 - k, x


def strip_kernel(blocks_ref, scales_ref, piece_ref):
    sub = lax.broadcasted_iota(jnp.int32, (16, BS), 0)
    rows = jnp.zeros((16, BS), jnp.float32)
    for a in range(4):
        for t, part in enumerate(split3(jnp.broadcast_to(scales_ref[a, 0:1, 0:1], (16, BS)))):
            rows = jnp.where(sub == 3 * a + t, part, rows)
    rows = rows.astype(jnp.bfloat16)
    for a in range(4):
        piece_ref[a * BS : (a + 1) * BS, :] = blocks_ref[a, :, 0, :]
    piece_ref[4 * BS :, :] = rows


def strip(blocks, scales):
    return pl.pallas_call(
        strip_kernel,
        grid=(1,),
        in_specs=[
            pl.BlockSpec((4, BS, 16, BS), lambda i: (0, 0, 0, 0)),
            pl.BlockSpec((4, 1, 32), lambda i: (0, 0, 0)),
        ],
        out_specs=pl.BlockSpec((PIECE, BS), lambda i: (0, 0)),
        out_shape=jax.ShapeDtypeStruct((PIECE, BS), jnp.bfloat16),
        compiler_params=pltpu.CompilerParams(vmem_limit_bytes=60 * 1024 * 1024),
        cost_estimate=pl.CostEstimate(flops=0, bytes_accessed=2 * 2**20, transcendentals=0),
        name="strip",
    )(blocks, scales)


def along_x(array, x):
    got = [
        permute(array, lambda z, y, k, x: (z, y, k, hop[x])) for hop in ((1, 0, 3, 2), (3, 2, 1, 0), (2, 3, 0, 1))
    ]
    return got


def by_column(array, got, x):
    u = jnp.where(x <= 1, array, got[1])
    v = jnp.where(x <= 1, got[0], got[2])
    return u, v


def trade(p, q):
    return (q if p == 0 else 0), p in (0, q)


def pick(at, zero, one, two, three):
    return jnp.where(at == 0, zero, jnp.where(at == 1, one, jnp.where(at == 2, two, three)))


def along_y(mine, y, x):
    def across(z, y, k, x):
        return (z, y + 2, k, x) if y % 2 == x // 2 else (z, y, 1 - k, x)

    up = permute(mine, lambda z, y, k, x: (z, y + 1, k, x))
    down = permute(mine, lambda z, y, k, x: (z, y - 1, k, x))
    over = permute(mine, across)
    turn = (y - x // 2) % 4
    slots = [pick(turn, mine, up, over, down), pick(turn, over, down, mine, up)]
    return jnp.concatenate(slots, axis=0)


def lead_along(pair, at, axis):
    got = []
    for q in (1, 2, 3):

        def place(*here):
            there = list(here)
            other, moves = trade(here[axis], q)
            there[axis if moves else 2] = other if moves else 1 - here[2]
            return there

        got.append(permute(pair, place))
    return pick(at, pair, *got)


def split3(x):
    h = x.astype(jnp.bfloat16).astype(jnp.float32)
    m = (x - h).astype(jnp.bfloat16).astype(jnp.float32)
    return h, m, x - h - m


def splat(x, shape):
    return jnp.broadcast_to(x, shape)


def eliminate(ref):
    width = ref.shape[1]
    lanes = width // BS
    wide = lambda w: jnp.concatenate([w] * lanes, axis=1)
    for base in range(0, BS, 16):
        tile = ref[base : base + 16, :]
        rows = [splat(tile[i : i + 1, :], (8, width)) for i in range(16)]
        cols = [splat(tile[:, base + j : base + j + 1], (16, BS)) for j in range(16)]
        e = [[splat(cols[j][i : i + 1, :], (8, BS)) for j in range(i + 1)] for i in range(16)]
        for j in range(16):
            r = lax.rsqrt(e[j][j])
            rows[j] = rows[j] * wide(r)
            l = [None] * 16
            for i in range(j + 1, 16):
                l[i] = e[i][j] * r
            for i in range(j + 1, 16):
                for m in range(j + 1, i + 1):
                    e[i][m] = e[i][m] - l[i] * l[m]
                rows[i] = rows[i] - wide(l[i]) * rows[j]
        sub = lax.broadcasted_iota(jnp.int32, (8, width), 0)
        out = []
        for g in range(0, 16, 8):
            acc = rows[g]
            for i in range(1, 8):
                acc = jnp.where(sub == i, rows[g + i], acc)
            out.append(acc)
        out = jnp.concatenate(out, axis=0)
        below = lax.broadcasted_iota(jnp.int32, (16, BS), 0) + base
        upper = jnp.where(lax.broadcasted_iota(jnp.int32, (16, BS), 1) >= below, out[:, :BS], 0.0)
        out = jnp.concatenate([upper, out[:, BS:]], axis=1)
        ref[base : base + 16, :] = out
        if base + 16 < BS:
            h, m, l = split3(out)
            left = jnp.concatenate([w[:, :BS] for w in (h, h, m, m, h, l)], axis=0).astype(jnp.bfloat16)
            right = jnp.concatenate([h, m, h, m, l, h], axis=0).astype(jnp.bfloat16)
            d = lax.dot_general(left, right, (((0,), (0,)), ((), ())), preferred_element_type=jnp.float32)
            ref[base + 16 :, :] = ref[base + 16 :, :] - d[base + 16 :, :]


def factor_kernel(place, pair_ref, other_ref, wk_ref, corner_ref, one_ref, two_ref):
    row, col, k = place[0], place[1], place[2]
    rows = BS + 16

    def value(ref, base):
        s = ref[base + BS : base + rows, :].astype(jnp.float32)
        s = s[0:1] + s[1:2] + s[2:3]
        return ref[base : base + BS, :].astype(jnp.float32) * s

    def fill(core0, core1):
        one_ref[:, :BS] = value(core0, 0)
        one_ref[:, BS : 2 * BS] = value(core1, 0).T
        two_ref[:, :BS] = value(core1, rows)

    @pl.when(k == 0)
    def _():
        fill(pair_ref, other_ref)

    @pl.when(k == 1)
    def _():
        fill(other_ref, pair_ref)

    e = lax.broadcasted_iota(jnp.int32, (BS, BS), 0)
    f = lax.broadcasted_iota(jnp.int32, (BS, BS), 1)
    eye = jnp.where(e == f, 1.0, 0.0)
    one_ref[:, 2 * BS :] = eye
    eliminate(one_ref)
    l10t = one_ref[:, BS : 2 * BS].astype(jnp.bfloat16)
    w00 = one_ref[:, 2 * BS :]
    inner = (((0,), (0,)), ((), ()))
    two_ref[:, :BS] = two_ref[:, :BS] - lax.dot_general(l10t, l10t, inner, preferred_element_type=jnp.float32)
    two_ref[:, BS : 2 * BS] = eye
    parts = jnp.concatenate(split3(w00), axis=0).astype(jnp.bfloat16)
    two_ref[:, 2 * BS :] = -lax.dot_general(
        jnp.concatenate([l10t] * 3, axis=0), parts, inner, preferred_element_type=jnp.float32
    )
    eliminate(two_ref)

    def put(h, r, w):
        hi = w.astype(jnp.bfloat16)
        wk_ref[h, r * BS : (r + 1) * BS, :BS] = hi
        wk_ref[h, r * BS : (r + 1) * BS, BS:] = (w - hi.astype(jnp.float32)).astype(jnp.bfloat16)

    put(0, 0, w00)
    put(0, 1, two_ref[:, 2 * BS :])
    put(1, 0, jnp.zeros((BS, BS), jnp.float32))
    put(1, 1, two_ref[:, BS : 2 * BS])

    corner_ref[...] = l10t.astype(jnp.float32)

    @pl.when((row == 0) & (col == 0))
    def _():
        corner_ref[...] = one_ref[:, :BS].T

    @pl.when((row == 1) & (col == 0))
    def _():
        corner_ref[...] = l10t.astype(jnp.float32).T

    @pl.when((row == 1) & (col == 1))
    def _():
        corner_ref[...] = two_ref[:, :BS].T


def factor(place, pair, other):
    return pl.pallas_call(
        factor_kernel,
        grid_spec=pltpu.PrefetchScalarGridSpec(
            num_scalar_prefetch=1,
            in_specs=[pl.BlockSpec(memory_space=pltpu.VMEM)] * 2,
            out_specs=[pl.BlockSpec(memory_space=pltpu.VMEM)] * 2,
            scratch_shapes=[pltpu.VMEM((BS, 3 * BS), jnp.float32)] * 2,
        ),
        out_shape=[
            jax.ShapeDtypeStruct((2, 2 * BS, 2 * BS), jnp.bfloat16),
            jax.ShapeDtypeStruct((BS, BS), jnp.float32),
        ],
        compiler_params=pltpu.CompilerParams(vmem_limit_bytes=16 * 1024 * 1024),
        cost_estimate=pl.CostEstimate(flops=10**6, bytes_accessed=2**16, transcendentals=0),
        name="factor",
    )(place, pair, other)


def finish_kernel(place, a_ref, sc_ref, m0, m1, m2, m3, t0, t1, t2, t3, u_ref, v_ref, wk_ref, corner_ref,
                  out_ref, big_ref, q_ref, p_ref, prod_ref):
    step = pl.program_id(0)
    row, col, k, z, first = place[0], place[1], place[2], place[3], place[4]

    def scale_of(ref, base, a):
        s = ref[base + 4 * BS : base + 4 * BS + 16, :].astype(jnp.float32)
        return s[3 * a : 3 * a + 1] + s[3 * a + 1 : 3 * a + 2] + s[3 * a + 2 : 3 * a + 3]

    def panel_tiles(ref_m, ref_t, base, a0, wm, wt):
        def part(ref, w):
            raw = ref[base + a0 * BS : base + (a0 + 2) * BS, :]
            d = lax.dot_general(
                jnp.concatenate([raw, raw], axis=1), w, (((1,), (1,)), ((), ())), preferred_element_type=jnp.float32
            )
            out = []
            for a in range(2):
                s = scale_of(ref, base, a0 + a)
                out.append(d[a * BS : (a + 1) * BS] * jnp.concatenate([s, s], axis=1))
            return out

        return [(g + h).astype(jnp.bfloat16) for g, h in zip(part(ref_m, wm), part(ref_t, wt))]

    @pl.when(step == 0)
    def _():
        w_mine = wk_ref[k]
        w_other = wk_ref[1 - k]
        for i, (mine, other) in enumerate(((m0, t0), (m1, t1), (m2, t2), (m3, t3))):
            zs = lax.rem(z + (0, 3, 1, 2)[i], 4)
            for ys in range(2):
                for a0 in range(0, 4, 2):
                    tiles = panel_tiles(mine, other, ys * PIECE, a0, w_mine, w_other)
                    for a, tile in enumerate(tiles):
                        b = (a0 + a) * 8 + zs * 2 + ys
                        q_ref[pl.ds(pl.multiple_of(b * BS, BS), BS), :] = tile
        w_u = wk_ref[first]
        w_v = wk_ref[1 - first]
        for a0 in range(0, 4, 2):
            for a, tile in enumerate(panel_tiles(u_ref, v_ref, 0, a0, w_u, w_v)):
                p_ref[(a0 + a) * BS : (a0 + a + 1) * BS, :] = tile
        e = lax.broadcasted_iota(jnp.int32, (BS, 2 * BS), 0)
        f = lax.broadcasted_iota(jnp.int32, (BS, 2 * BS), 1)

        @pl.when(row < 2)
        def _():
            p_ref[0:BS, :] = jnp.where(f == e + row * BS, -1.0, 0.0).astype(jnp.bfloat16)

        @pl.when(col < 2)
        def _():
            q_ref[0:BS, :] = jnp.where(f == e + col * BS, -1.0, 0.0).astype(jnp.bfloat16)

    p = p_ref[pl.ds(pl.multiple_of(step * BS, BS), BS), :]
    for b in range(32):
        d = lax.dot_general(
            p, q_ref[b * BS : (b + 1) * BS, :], (((1,), (1,)), ((), ())), preferred_element_type=jnp.float32
        )
        prod_ref[pl.ds(b, BS, stride=40), :] = d

    @pl.when((step == 0) & (row < 2) & (col < 2))
    def _():
        prod_ref[pl.ds(0, BS, stride=40), :] = -corner_ref[...]

    sc = sc_ref[0]

    def update(e, mx):
        rows = pl.ds(pl.multiple_of(e * 40, 8), 32)
        m = a_ref[0, e].astype(jnp.float32) * sc - prod_ref[rows, :]
        prod_ref[rows, :] = m
        return jnp.maximum(mx, jnp.abs(m))

    mx = lax.fori_loop(0, BS, update, jnp.zeros((32, BS), jnp.float32), unroll=8)
    big = jnp.max(mx, axis=1, keepdims=True) + 1e-06
    big = jnp.broadcast_to(big, (32, BS))
    big_ref[0] = big.T[0:1]
    inv = 1.0 / big

    def divide(e, carry):
        rows = pl.ds(pl.multiple_of(e * 40, 8), 32)
        out_ref[0, e] = (prod_ref[rows, :] * inv).astype(jnp.bfloat16)
        return carry

    lax.fori_loop(0, BS, divide, 0, unroll=8)


def finish(place, blocks, sc, held, others, u, v, wk, corner):
    whole = lambda shape: pl.BlockSpec(memory_space=pltpu.VMEM)
    spec = pltpu.PrefetchScalarGridSpec(
        num_scalar_prefetch=1,
        grid=(4,),
        in_specs=[
            pl.BlockSpec((1, BS, 32, BS), lambda a, *_: (a, 0, 0, 0)),
            pl.BlockSpec((1, 32, BS), lambda a, *_: (a, 0, 0)),
        ]
        + [whole((2 * PIECE, BS))] * 8
        + [whole((PIECE, BS))] * 2
        + [whole((2, 2 * BS, 2 * BS)), whole((BS, BS))],
        out_specs=[
            pl.BlockSpec((1, BS, 32, BS), lambda a, *_: (a, 0, 0, 0)),
            pl.BlockSpec((1, 1, 32), lambda a, *_: (a, 0, 0)),
        ],
        scratch_shapes=[
            pltpu.VMEM((32 * BS, 2 * BS), jnp.bfloat16),
            pltpu.VMEM((4 * BS, 2 * BS), jnp.bfloat16),
            pltpu.VMEM((40 * BS, BS), jnp.float32),
        ],
    )
    return pl.pallas_call(
        finish_kernel,
        grid_spec=spec,
        out_shape=[
            jax.ShapeDtypeStruct((4, BS, 32, BS), jnp.bfloat16),
            jax.ShapeDtypeStruct((4, 1, 32), jnp.float32),
        ],
        compiler_params=pltpu.CompilerParams(vmem_limit_bytes=32 * 1024 * 1024),
        cost_estimate=pl.CostEstimate(flops=2 * 512 * 4096 * 512, bytes_accessed=12 * 2**20, transcendentals=0),
        name="finish",
    )(place, blocks, sc, *held, *others, u, v, wk, corner)


def on_device(blocks, scales):
    row = lax.axis_index("row")
    col = lax.axis_index("col")
    x = col
    k = row % 2
    y = (row // 2) % 4
    z = row // 8
    blocks = blocks.reshape(4, BS, 32, BS)
    scales = scales.reshape(4, 32)
    piece = strip(blocks, scales.reshape(4, 1, 32))
    first = jnp.where((x == 0) | (x == 3), 0, 1)
    place = jnp.stack([row, col, k, z, first]).astype(jnp.int32)
    got = along_x(piece, x)
    u, v = by_column(piece, got, x)
    ours = jnp.where(x <= 1, piece, got[2])
    mine = jnp.where(k == x % 2, ours, permute(jnp.where(x <= 1, got[0], got[1]), sibling))
    head = lambda w: jnp.concatenate([w[:BS], w[4 * BS :]], axis=0)
    pair = jnp.concatenate([jnp.where(first == 0, head(u), head(v)), jnp.where(first == 0, head(v), head(u))], axis=0)
    pair = lead_along(pair, y, 1)
    both = along_y(mine, y, x)
    pair = lead_along(pair, z, 0)
    pair, piece, got = lax.optimization_barrier((pair, piece, got))
    u, v = by_column(piece, got, x)
    held = [both] + [permute(both, lambda z, y, k, x: (z + d, y, k, x)) for d in (1, -1, 2)]
    wk, corner = factor(place, pair, permute(pair, sibling))
    wk, *held[1:] = lax.optimization_barrier((wk, *held[1:]))
    others = [permute(h, sibling) for h in held]
    special = ((jnp.arange(4) == 0) & (row < 2))[:, None] | ((jnp.arange(32) == 0) & (col < 2))[None, :]
    sc = jnp.broadcast_to(jnp.where(special, 0.0, scales)[:, :, None], (4, 32, BS))
    factored, largest = finish(place, blocks, sc, held, others, u, v, wk, corner)
    return factored.reshape(4, 1, BS, 32, 1, BS), largest.reshape(4, 1, 32, 1)


def solution(mesh):
    in_specs = (P(None, "row", None, None, "col", None), P(None, "row", None, "col"))
    out_specs = (P(None, "row", None, None, "col", None), P(None, "row", None, "col"))
    return jax.shard_map(
        on_device, mesh=mesh, in_specs=in_specs, out_specs=out_specs, check_vma=False
    )
```
